32 devices in a mesh: groups: 2 (over x), seq: 16 (over z, y, core).
Axes of the slice: x: 2, y: 2, z: 4, core: 2. Of those that a mesh axis runs over, the one named last changes fastest.
Arguments:
- tokens: bfloat16 [12288, 5120], P(('groups', 'seq')), parts along dimension 0, may hold values from -6 to 6
- token_adapter_index: int32 [12288], P(('groups', 'seq')), parts along dimension 0, may hold values from 0 to 7
- frozen_value_weight: bfloat16 [5120, 1024], P('seq'), may hold values from -0.078125 to 0.078125
- weight_block_scale: float32 [40, 8], replicated, may hold values from 0.5 to 2
- down_adapter_weight: bfloat16 [10240, 128], P('groups'), parts along dimension 0, may hold values from -0.078125 to 0.078125
- up_adapter_weight: bfloat16 [256, 1024], P('groups'), parts along dimension 0, may hold values from -1.5 to 1.5
- cotangent: bfloat16 [12288, 1024], P(('groups', 'seq')), parts along dimension 0, may hold values from -6 to 6
Outputs:
- values: bfloat16 [12288, 1024], P(('groups', 'seq')), parts along dimension 0
- activation_gradient: bfloat16 [12288, 5120], P(('groups', 'seq')), parts along dimension 0
- grad_a: float32 [10240, 128], P(('groups', 'seq')), parts along dimension 0
- grad_b: float32 [256, 1024], P('groups'), parts along dimension 0
The draws below stay inside these ranges and needn't reach their ends.
There are 2 independent parts, one for each index of `groups`. The reference program is written for one: setup_inputs(seed, part) draws one part's arguments, and reference() takes and returns one part's arrays. A program takes and returns all parts, laid end to end along the dimension named above; an argument that names none is the same for every part. Nothing has to cross between parts.
All inputs are finite; a program needn't handle non-finite values.
Results may differ from the reference program's by a relative error of at most 0.005.
Values may be sent and summed in bfloat16 or wider, within the bound.
No kernel may reach another device: no remote copies, remote signals or barrier semaphores. Data moves between devices by JAX's collectives and lax.ppermute only.
A program may use at most 128 MiB of HBM per device.

```python
import math
import jax
import jax.numpy as jnp
import numpy as np
from jax import lax

MODEL_WIDTH = 5120
VALUE_WIDTH = 1024
BLOCK = 128
ADAPTERS = 8
ADAPTER_RANK = 16
ALL_ADAPTER_RANK = 128
TOKENS = 6144


def place_ends(values, stream_key, smallest, largest):
    shape = values.shape
    spot = [jax.random.randint(jax.random.fold_in(stream_key, axis), (), 0, shape[axis]) for axis in range(len(shape))]
    values = values.at[tuple(spot)].set(smallest)
    longest = shape.index(max(shape))
    spot[longest] = (spot[longest] + 1) % shape[longest]
    return values.at[tuple(spot)].set(largest)


def spiked(values, rng, source, target, blocks, factor):
    def block_of(dim):
        return (jnp.arange(values.shape[dim]) // (values.shape[dim] // blocks)).reshape((-1,) + (1,) * (values.ndim - 1 - dim))

    first = jax.random.permutation(rng, blocks)[block_of(target)]
    second = (block_of(target) + blocks // 2) % blocks
    return jnp.where((block_of(source) == first) | (block_of(source) == second), factor * values, values)


def shard_levels(key, shape, split, low, largest):
    factor_of, own = 1.0, jax.random.fold_in(key, 6)
    for dim, blocks in split:
        heights = jnp.exp(jax.random.uniform(jax.random.fold_in(own, dim), (blocks,), jnp.float32, low / len(split), largest / len(split)))
        factor_of = factor_of * jnp.repeat(heights, shape[dim] // blocks).reshape([-1 if axis == dim else 1 for axis in range(len(shape))])
    return factor_of


def rank_table(count, slope):
    portions = [(1 << 20) // math.isqrt(grade ** slope) + 1 for grade in range(1, count + 1)]
    width = 1 + sum(portions) // (1 << 30)
    return np.cumsum(np.array([max(1, weight // width) for weight in portions]))


def ranked_ids(key, shape, amount, skew):
    table = rank_table(amount, skew)
    pick = jax.random.randint(jax.random.fold_in(key, 1), shape, 0, int(table[amount - 1]))
    standing = jnp.searchsorted(jnp.asarray(table, jnp.int32), pick, side="right")
    return jax.random.permutation(jax.random.fold_in(key, 2), amount)[standing].astype(jnp.int32)


def bell_draw(key, dims, scale, reach, cuts=(), dtype=jnp.bfloat16):
    entries = scale * jax.random.normal(key, dims, jnp.float32)
    if cuts:
        entries = entries * shard_levels(key, dims, cuts, -0.22, 0.18)
    return jnp.clip(entries, -reach, reach).astype(dtype)


def heavy_noise(rng, dims, width, most, split, heavy, kind=jnp.bfloat16):
    result = width * jax.random.normal(rng, dims, jnp.float32)
    if split:
        result = result * shard_levels(rng, dims, split, -0.22, 0.18)
    return jnp.clip(spiked(result, jax.random.fold_in(rng, 3), *heavy), -most, most).astype(kind)


def setup_inputs(seed: int = 0, part: int = 0) -> dict:
    key_of = jax.random.split(jax.random.key(seed), 8)
    part_keys = jax.random.split(jax.random.fold_in(key_of[7], part), 8)
    tokens = heavy_noise(part_keys[0], (TOKENS, MODEL_WIDTH), 1.0, 6.0, ((0, 16),), (0, 1, 16, 2.0))
    token_adapter_index = place_ends(ranked_ids(part_keys[1], (TOKENS,), ADAPTERS, 2), jax.random.fold_in(part_keys[1], 3), 0, ADAPTERS - 1).astype(jnp.int32)
    frozen_value_weight = bell_draw(key_of[2], (MODEL_WIDTH, VALUE_WIDTH), MODEL_WIDTH ** -0.5, 0.078125, ((0, 16),))
    weight_block_scale = jnp.clip(jnp.exp(jax.random.uniform(key_of[3], (MODEL_WIDTH // BLOCK, VALUE_WIDTH // BLOCK), jnp.float32, math.log(0.5), math.log(2.0))), 0.5, 2.0)
    down_adapter_weight = bell_draw(part_keys[4], (MODEL_WIDTH, ALL_ADAPTER_RANK), MODEL_WIDTH ** -0.5, 0.078125)
    up_adapter_weight = bell_draw(part_keys[5], (ALL_ADAPTER_RANK, VALUE_WIDTH), ADAPTER_RANK ** -0.5, 1.5)
    cotangent = bell_draw(part_keys[6], (TOKENS, VALUE_WIDTH), 1.0, 6.0, ((0, 16),))
    return dict(tokens=tokens, token_adapter_index=token_adapter_index, frozen_value_weight=frozen_value_weight, weight_block_scale=weight_block_scale, down_adapter_weight=down_adapter_weight, up_adapter_weight=up_adapter_weight, cotangent=cotangent)


def dequantize(quant, scales):
    nrow, ncol = quant.shape
    blocks = quant.astype(jnp.float32).reshape(nrow // BLOCK, BLOCK, ncol // BLOCK, BLOCK)
    blocks = blocks * scales[:, None, :, None]
    return blocks.reshape(nrow, ncol).astype(jnp.bfloat16)


def reference(tokens, token_adapter_index, frozen_value_weight, weight_block_scale, down_adapter_weight, up_adapter_weight, cotangent):
    weight = dequantize(frozen_value_weight, weight_block_scale)
    token_adapter_mask = lax.iota(jnp.int32, ADAPTERS * ADAPTER_RANK) // ADAPTER_RANK
    adapter_choice_mask = (token_adapter_index[:, None] == token_adapter_mask[None, :]).astype(jnp.float32)
    down_projected = (jnp.dot(tokens, down_adapter_weight, preferred_element_type=jnp.float32) * adapter_choice_mask).astype(jnp.bfloat16)
    values = jnp.dot(tokens, weight, preferred_element_type=jnp.float32)
    values = (values + 2.0 * jnp.dot(down_projected, up_adapter_weight, preferred_element_type=jnp.float32)).astype(jnp.bfloat16)
    expanded_rank_mask = 2.0 * jnp.dot(cotangent, up_adapter_weight.T, preferred_element_type=jnp.float32) * adapter_choice_mask
    expanded_rank_mask = expanded_rank_mask.astype(jnp.bfloat16)
    activation_gradient = jnp.dot(cotangent, weight.T, preferred_element_type=jnp.float32)
    activation_gradient = (activation_gradient + jnp.dot(expanded_rank_mask, down_adapter_weight.T, preferred_element_type=jnp.float32)).astype(jnp.bfloat16)
    grad_a = jnp.dot(tokens.T, expanded_rank_mask, preferred_element_type=jnp.float32)
    grad_b = 2.0 * jnp.dot(down_projected.T, cotangent, preferred_element_type=jnp.float32)
    return values, activation_gradient, grad_a, grad_b
```

```python
import functools

import jax
import jax.numpy as jnp
from jax import lax
from jax.experimental import pallas as pl
from jax.experimental.pallas import tpu as pltpu
from jax.sharding import PartitionSpec as P

BLOCK = 128
ADAPTER_RANK = 16
STRIP = 64
VMEM_LIMIT = 48 * 1024 * 1024
F32 = jnp.float32
BF16 = jnp.bfloat16


def dequant_rows(piece, scales):
    count = piece.shape[0]
    block_of = lax.iota(jnp.int32, count) // BLOCK
    select = (block_of[:, None] == lax.iota(jnp.int32, scales.shape[0])[None, :]).astype(F32)
    row_scales = jnp.dot(select, scales, precision=lax.Precision.HIGHEST)
    expanded = jnp.repeat(row_scales, BLOCK, axis=1)
    return (piece.astype(F32) * expanded).astype(BF16)


def reduce_over_rows(left, right):
    return lax.dot_general(left, right, (((1,), (1,)), ((), ())), preferred_element_type=F32)


def contract_tokens(left, right):
    return lax.dot_general(left, right, (((0,), (0,)), ((), ())), preferred_element_type=F32)


def plain_path(tokens, token_adapter_index, frozen, scales, down, up, cotangent):
    rank_adapter = lax.iota(jnp.int32, down.shape[1]) // ADAPTER_RANK
    mask = (token_adapter_index[:, None] == rank_adapter[None, :]).astype(F32)
    shrink = (jnp.dot(tokens, down, preferred_element_type=F32) * mask).astype(BF16)
    spread = (2.0 * reduce_over_rows(cotangent, up) * mask).astype(BF16)
    weight = dequant_rows(lax.all_gather(frozen, "seq", axis=0, tiled=True), scales)
    values = jnp.dot(tokens, weight, preferred_element_type=F32)
    values = (values + 2.0 * jnp.dot(shrink, up, preferred_element_type=F32)).astype(BF16)
    act = reduce_over_rows(cotangent, weight) + reduce_over_rows(spread, down)
    grad_a = lax.psum_scatter(
        contract_tokens(tokens, spread), "seq", scatter_dimension=0, tiled=True
    )
    grad_b = lax.psum(2.0 * contract_tokens(shrink, cotangent), "seq")
    return values, act.astype(BF16), grad_a, grad_b


def call(body, name, grid, in_specs, out_specs, out_shape, scratch=(), alias=None, cost=None):
    return pl.pallas_call(
        body,
        name=name,
        grid_spec=pltpu.PrefetchScalarGridSpec(
            num_scalar_prefetch=1,
            grid=grid,
            in_specs=in_specs,
            out_specs=out_specs,
            scratch_shapes=scratch,
        ),
        out_shape=out_shape,
        input_output_aliases=alias or {},
        compiler_params=pltpu.CompilerParams(vmem_limit_bytes=VMEM_LIMIT),
        cost_estimate=cost,
    )


def whole(shape):
    return pl.BlockSpec(shape, lambda *_: (0,) * len(shape))


def struct(shape, dtype):
    return jax.ShapeDtypeStruct(shape, dtype)


def dequant_body(info, w, scales, shared, rest):
    z, y, c, x = info[0], info[1], info[2], info[3]
    strips = w.shape[0] // STRIP
    first = ((z * 2 + y) * 2 + c) * strips
    kept = rest.shape[0] // STRIP
    middle = strips - 2 * kept

    def scale_strip(out, at, source):
        block_row = lax.div((first + source) * STRIP, BLOCK)
        rows = pl.ds(pl.multiple_of(source * STRIP, STRIP), STRIP)
        for b in range(w.shape[1] // BLOCK):
            columns = pl.ds(b * BLOCK, BLOCK)
            value = w[rows, columns].astype(F32) * scales[block_row, b]
            out[pl.ds(at * STRIP, STRIP), columns] = value.astype(BF16)

    for i in range(kept):
        scale_strip(shared, i, x * (kept + middle) + i)
        scale_strip(rest, i, (1 - x) * (kept + middle) + i)
    for i in range(middle):
        scale_strip(shared, kept + i, kept + i)


def grads_body(steps, rows, info, tok, idx, down, up, cot, shrink, spread, send, keep, acc):
    j = pl.program_id(0)
    c = info[2]
    ranks = up.shape[0]
    rank_adapter = lax.broadcasted_iota(jnp.int32, (1, ranks), 1) // ADAPTER_RANK
    mask = (idx[...] == rank_adapter).astype(F32)

    @pl.when(j == 0)
    def _():
        spread[...] = (2.0 * reduce_over_rows(cot[...], up[...]) * mask).astype(BF16)
        acc[...] = jnp.zeros_like(acc)

    acc[...] += jnp.dot(tok[...], down[...], preferred_element_type=F32)
    part = contract_tokens(tok[...], spread[...])

    def place(own, other):
        for y in range(2):
            for core in range(2):
                at = (y * 2 + core) * rows
                out = (own, other)[core]
                out[j, y, pl.ds(0, rows), :] = part[at : at + rows]

    @pl.when(c == 0)
    def _():
        place(keep, send)

    @pl.when(c == 1)
    def _():
        place(send, keep)

    @pl.when(j == steps - 1)
    def _():
        shrink[...] = (acc[...] * mask).astype(BF16)
        grad_b = contract_tokens(shrink[...], cot[...])
        half = ranks // 2

        def place_b(own, other):
            for zz in range(steps):
                for y in range(2):
                    for core in range(2):
                        column = (zz * 2 + y) * ranks
                        piece = grad_b[core * half : (core + 1) * half, column : column + ranks]
                        (own, other)[core][zz, y, pl.ds(rows, half), :] = piece

        @pl.when(c == 0)
        def _():
            place_b(keep, send)

        @pl.when(c == 1)
        def _():
            place_b(send, keep)


def pair_body(info, keep, got, own, s1, s2, s3):
    j = pl.program_id(0)
    total = keep[0] + got[0]

    @pl.when(j == 0)
    def _():
        own[...] = total

    for step, out in ((1, s1), (2, s2), (3, s3)):

        @pl.when(j == step)
        def _(out=out):
            out[...] = total.astype(BF16)


def line_body(info, own, r1, r2, r3, mine, other):
    y = info[1]

    def total(at):
        return (
            own[at] + r1[at].astype(F32) + r2[at].astype(F32) + r3[at].astype(F32)
        )

    mine[...] = total(y)
    other[...] = total(1 - y).astype(BF16)


def last_body(info, mine, got, grad_a, piece_b):
    rows = grad_a.shape[0]
    total = mine[...] + got[...].astype(F32)
    grad_a[...] = total[:rows]
    piece_b[...] = 2.0 * total[rows:]


def place_b_body(info, own, other, out):
    z, y, c = info[0], info[1], info[2]
    half, ranks = own.shape[2:]
    for from_core, ref in ((c, own), (1 - c, other)):
        for i in range(2):
            yy = y if i == 0 else 1 - y
            for k in range(own.shape[1]):
                zz = lax.rem(z + 4 - k, 4)
                column = pl.multiple_of((zz * 2 + yy) * ranks, ranks)
                row = pl.multiple_of(from_core * half, half)
                out[pl.ds(row, half), pl.ds(column, ranks)] = ref[i, k]


def plane_body(first, last, rows, info, tok, cot, spread, down, *refs):
    pieces, refs = refs[:8], refs[8:]
    if first:
        shrink, up, act, acc, weight = refs
    else:
        total, _, act, acc, weight = refs
    y, c, x = info[1], info[2], info[3]
    for i, yy in enumerate((y, 1 - y)):
        for h, cc in enumerate((c, 1 - c)):
            shared, rest = pieces[h * 4 + i * 2], pieces[h * 4 + i * 2 + 1]
            base = (yy * 2 + cc) * rows
            kept = rest.shape[0]
            middle = shared.shape[0] - kept
            at = pl.multiple_of(base + x * (kept + middle), STRIP)
            weight[pl.ds(at, kept), :] = shared[:kept]
            at = pl.multiple_of(base + kept, STRIP)
            weight[pl.ds(at, middle), :] = shared[kept:]
            at = pl.multiple_of(base + (1 - x) * (kept + middle), STRIP)
            weight[pl.ds(at, kept), :] = rest[...]
    forward = jnp.dot(tok[...], weight[...], preferred_element_type=F32)
    if first:
        forward += 2.0 * jnp.dot(shrink[...], up[...], preferred_element_type=F32)
    else:
        forward += total[...]
    acc[...] = forward.astype(acc.dtype)
    back = reduce_over_rows(cot[...], weight[...]) + reduce_over_rows(spread[...], down[...])
    act[...] = back.astype(BF16)


def swap(n, move):
    pairs = []
    for s in range(n):
        z, y, c = move(s // 4, s // 2 % 2, s % 2)
        pairs.append((s, (z % (n // 4) * 2 + y) * 2 + c))
    return pairs


def block_path(tokens, token_adapter_index, frozen, scales, down, up, cotangent):
    n, planes = 16, 4
    count, width = tokens.shape
    rows, columns = frozen.shape
    ranks = up.shape[0]
    depth = width // planes
    kept = rows * 2 // 5 // STRIP * STRIP
    shared_rows = rows - kept
    half = ranks // 2
    piece_rows = rows + half

    s = lax.axis_index("seq").astype(jnp.int32)
    x = lax.axis_index("groups").astype(jnp.int32)
    info = jnp.stack([s // 4, s // 2 % 2, s % 2, x])

    def over_z(v, by=1):
        return lax.ppermute(v, "seq", swap(n, lambda z, y, c: (z + by, y, c)))

    def over_y(v):
        return lax.ppermute(v, "seq", swap(n, lambda z, y, c: (z, 1 - y, c)))

    def over_core(v):
        return lax.ppermute(v, "seq", swap(n, lambda z, y, c: (z, y, 1 - c)))

    def over_x(v):
        return lax.ppermute(v, "groups", [(0, 1), (1, 0)])

    shared, rest = call(
        dequant_body,
        "scale_rows",
        (1,),
        [whole((rows, columns)), pl.BlockSpec(memory_space=pltpu.SMEM)],
        [whole((shared_rows, columns)), whole((kept, columns))],
        [struct((shared_rows, columns), BF16), struct((kept, columns), BF16)],
    )(info, frozen, scales)

    near = [shared]
    for _ in range(1, planes):
        near.append(over_z(near[-1]))
    far = [over_y(v) for v in near]
    near_rest = [rest] + [over_x(v[:kept]) for v in near[1:]]
    far_rest = [over_x(v[:kept]) for v in far]

    piece = (planes, 2, piece_rows, ranks)
    shrink, spread, send, keep = call(
        functools.partial(grads_body, planes, rows),
        "gradient_shares",
        (planes,),
        [
            pl.BlockSpec((count, depth), lambda j, _: (0, j)),
            whole((count, 1)),
            pl.BlockSpec((depth, ranks), lambda j, _: (j, 0)),
            whole((ranks, columns)),
            whole((count, columns)),
        ],
        [whole((count, ranks)), whole((count, ranks)), whole(piece), whole(piece)],
        [
            struct((count, ranks), BF16),
            struct((count, ranks), BF16),
            struct(piece, F32),
            struct(piece, F32),
        ],
        scratch=[pltpu.VMEM((count, ranks), F32)],
    )(info, tokens, token_adapter_index[:, None], down, up, cotangent)

    pair = (2, piece_rows, ranks)
    block = pl.BlockSpec((1,) + pair, lambda j, info: (lax.rem(info[0] + j, 4), 0, 0, 0))
    own, s1, s2, s3 = call(
        pair_body,
        "add_core",
        (planes,),
        [block, block],
        [whole(pair)] * 4,
        [struct(pair, F32)] + [struct(pair, BF16)] * 3,
    )(info, keep, over_core(send))
    mine, other = call(
        line_body,
        "add_line",
        (1,),
        [whole(pair)] * 4,
        [whole(pair[1:])] * 2,
        [struct(pair[1:], F32), struct(pair[1:], BF16)],
    )(info, own, over_z(s1, 1), over_z(s2, 2), over_z(s3, 3))
    grad_a, piece_b = call(
        last_body,
        "add_side",
        (1,),
        [whole(pair[1:])] * 2,
        [whole((rows, ranks)), whole((half, ranks))],
        [struct((rows, ranks), F32), struct((half, ranks), F32)],
    )(info, mine, over_y(other))
    line_b = jnp.stack([piece_b] + [over_z(piece_b, k) for k in range(1, planes)])
    side_b = jnp.stack([line_b, over_y(line_b)])
    grad_b = call(
        place_b_body,
        "place_up_gradient",
        (1,),
        [whole(side_b.shape)] * 2,
        whole((ranks, columns)),
        struct((ranks, columns), F32),
    )(info, side_b, over_core(side_b))

    act = total = None
    for k in range(planes):
        mine_k = [near[k], near_rest[k], far[k], far_rest[k]]
        pieces = mine_k + [over_core(v) for v in mine_k]
        first, last = k == 0, k == planes - 1
        at = functools.partial(lambda k, j, info: lax.rem(info[0] + 4 - k, 4), k)
        in_specs = [
            pl.BlockSpec((count, depth), lambda j, info, at=at: (0, at(j, info))),
            whole((count, columns)),
            whole((count, ranks)),
            pl.BlockSpec((depth, ranks), lambda j, info, at=at: (at(j, info), 0)),
        ] + [whole(v.shape) for v in pieces]
        operands = [tokens, cotangent, spread, down] + pieces
        if first:
            in_specs += [whole((count, ranks)), whole((ranks, columns))]
            operands += [shrink, up]
            alias = None
        else:
            in_specs += [whole((count, columns)), pl.BlockSpec(memory_space=pl.ANY)]
            operands += [total, act]
            alias = {len(operands): 0}
        act, total = call(
            functools.partial(plane_body, first, last, rows),
            f"plane_{k}",
            (1,),
            in_specs,
            [in_specs[0], whole((count, columns))],
            [struct((count, width), BF16), struct((count, columns), BF16 if last else F32)],
            scratch=[pltpu.VMEM((depth, columns), BF16)],
            alias=alias,
            cost=pl.CostEstimate(
                flops=4 * count * depth * columns,
                bytes_accessed=8 * 1024 * 1024,
                transcendentals=0,
            ),
        )(info, *operands)
    return total, act, grad_a, grad_b


def solution(mesh):
    sizes = (mesh.shape["groups"], mesh.shape["seq"])

    def on_device(*operands):
        rows, columns = operands[2].shape
        ranks = operands[5].shape[0]
        fits = rows % STRIP == 0 and rows >= 5 * STRIP and columns == 8 * ranks
        path = block_path if sizes == (2, 16) and fits and ranks == BLOCK else plain_path
        return path(*operands)

    return jax.shard_map(
        on_device,
        mesh=mesh,
        in_specs=(
            P(("groups", "seq"), None),
            P(("groups", "seq")),
            P("seq", None),
            P(),
            P("groups", None),
            P("groups", None),
            P(("groups", "seq"), None),
        ),
        out_specs=(
            P(("groups", "seq"), None),
            P(("groups", "seq"), None),
            P(("groups", "seq"), None),
            P("groups", None),
        ),
        check_vma=False,
    )
```

```python
import functools

import jax
import jax.numpy as jnp
from jax import lax
from jax.experimental import pallas as pl
from jax.experimental.pallas import tpu as pltpu
from jax.sharding import PartitionSpec as P

BLOCK = 128
ADAPTER_RANK = 16
STRIP = 64
VMEM_LIMIT = 12 * 1024 * 1024
F32 = jnp.float32
BF16 = jnp.bfloat16


def dequant_rows(piece, scales):
    count = piece.shape[0]
    block_of = lax.iota(jnp.int32, count) // BLOCK
    select = (block_of[:, None] == lax.iota(jnp.int32, scales.shape[0])[None, :]).astype(F32)
    row_scales = jnp.dot(select, scales, precision=lax.Precision.HIGHEST)
    expanded = jnp.repeat(row_scales, BLOCK, axis=1)
    return (piece.astype(F32) * expanded).astype(BF16)


def reduce_over_rows(left, right):
    return lax.dot_general(left, right, (((1,), (1,)), ((), ())), preferred_element_type=F32)


def contract_tokens(left, right):
    return lax.dot_general(left, right, (((0,), (0,)), ((), ())), preferred_element_type=F32)


def plain_path(tokens, token_adapter_index, frozen, scales, down, up, cotangent):
    rank_adapter = lax.iota(jnp.int32, down.shape[1]) // ADAPTER_RANK
    mask = (token_adapter_index[:, None] == rank_adapter[None, :]).astype(F32)
    shrink = (jnp.dot(tokens, down, preferred_element_type=F32) * mask).astype(BF16)
    spread = (2.0 * reduce_over_rows(cotangent, up) * mask).astype(BF16)
    weight = dequant_rows(lax.all_gather(frozen, "seq", axis=0, tiled=True), scales)
    values = jnp.dot(tokens, weight, preferred_element_type=F32)
    values = (values + 2.0 * jnp.dot(shrink, up, preferred_element_type=F32)).astype(BF16)
    act = reduce_over_rows(cotangent, weight) + reduce_over_rows(spread, down)
    grad_a = lax.psum_scatter(
        contract_tokens(tokens, spread), "seq", scatter_dimension=0, tiled=True
    )
    grad_b = lax.psum(2.0 * contract_tokens(shrink, cotangent), "seq")
    return values, act.astype(BF16), grad_a, grad_b


GAP = 60
VMEM = pl.BlockSpec(memory_space=pltpu.VMEM)
SMEM = pl.BlockSpec(memory_space=pltpu.SMEM)
ANY = pl.BlockSpec(memory_space=pl.ANY)
HBM = pl.BlockSpec(memory_space=pltpu.HBM)


def struct(shape, dtype):
    return jax.ShapeDtypeStruct(shape, dtype)


def kernel(body, name, us, out_shape, in_specs, out_specs, operands, scratch=(), alias=None):
    return pl.pallas_call(
        body,
        name=name,
        in_specs=in_specs,
        out_specs=out_specs,
        out_shape=out_shape,
        scratch_shapes=scratch,
        input_output_aliases=alias or {},
        compiler_params=pltpu.CompilerParams(vmem_limit_bytes=VMEM_LIMIT),
        cost_estimate=pl.CostEstimate(
            flops=int(us * 1.1e9), bytes_accessed=1, transcendentals=0
        ),
    )(*operands)


def after(value, *others):
    return lax.optimization_barrier((value,) + others)[0]


def place():
    s = lax.axis_index("seq")
    return s // 4, s // 2 % 2, s % 2, lax.axis_index("groups")


def strip_places(core, x):
    low = core * STRIP
    return low + x * (2 * STRIP), (1 - core) * (4 * STRIP), low + (1 - x) * (2 * STRIP)


def fetch(pairs, sems):
    copies = [pltpu.make_async_copy(a, b, sems.at[i]) for i, (a, b) in enumerate(pairs)]
    for copy in copies:
        copy.start()
    return copies


def dequant_body(w_far, scales_far, shared, rest, w, scales, sems):
    for copy in fetch(((scales_far, scales), (w_far, w)), sems):
        copy.wait()
    z, y, c, x = place()
    first = ((z * 2 + y) * 2 + c) * (w.shape[0] // STRIP)

    def scale_strips(out, at, count, source):
        for i in range(count // STRIP):
            start = source + i * STRIP
            block_row = (first * STRIP + start) // BLOCK
            rows = pl.ds(pl.multiple_of(start, STRIP), STRIP)
            for b in range(w.shape[1] // BLOCK):
                columns = pl.ds(b * BLOCK, BLOCK)
                value = w[rows, columns].astype(F32) * scales[b, block_row]
                out[pl.ds(at + i * STRIP, STRIP), columns] = value.astype(BF16)

    kept = rest.shape[0]
    mine, middle, other = strip_places(c, x)
    scale_strips(shared, 0, kept, mine)
    scale_strips(shared, kept, shared.shape[0] - kept, middle)
    scale_strips(rest, 0, kept, other)


def grads_body(rows, tok_far, idx, down_far, up_far, cot_far, _, *refs):
    shrink, spread, send, keep, tok, down, up, cot, acc, sems = refs
    c = place()[2]
    ranks, planes = up.shape[0], send.shape[0]
    depth = tok.shape[1] // planes
    half = ranks // 2
    pairs = [(up_far, up), (cot_far, cot)]
    for j in range(planes):
        part = pl.ds(j * depth, depth)
        pairs += [(tok_far.at[:, part], tok.at[:, part]), (down_far.at[part, :], down.at[part, :])]
    copies = fetch(pairs, sems)
    rank_adapter = lax.broadcasted_iota(jnp.int32, (ranks, 1), 0) // ADAPTER_RANK
    mask = (idx[...] == rank_adapter).astype(F32).T
    copies[0].wait()
    copies[1].wait()
    spread[...] = (2.0 * reduce_over_rows(cot[...], up[...]) * mask).astype(BF16)

    def store(j, y, core, at, value):
        @pl.when(c == core)
        def _():
            keep[j, y, pl.ds(at, value.shape[0]), :] = value

        @pl.when(c != core)
        def _():
            send[j, y, pl.ds(at, value.shape[0]), :] = value

    for j in range(planes):
        copies[2 + 2 * j].wait()
        copies[3 + 2 * j].wait()
        block = tok[:, j * depth : (j + 1) * depth]
        sum_j = jnp.dot(block, down[j * depth : (j + 1) * depth], preferred_element_type=F32)
        if j == 0:
            acc[...] = sum_j
        else:
            acc[...] += sum_j
        part = contract_tokens(block, spread[...])
        for y in range(2):
            for core in range(2):
                at = (y * 2 + core) * rows
                store(j, y, core, 0, part[at : at + rows])
    shrink[...] = (acc[...] * mask).astype(BF16)
    grad_b = contract_tokens(shrink[...], cot[...])
    for y in range(2):
        for j in range(planes):
            at = (y * planes + j) * ranks
            for core in range(2):
                piece = grad_b[core * half : (core + 1) * half, at : at + ranks]
                store(j, y, core, rows, piece)


def core_sum_body(keep, got, own, other):
    y = place()[1]
    for j in range(keep.shape[0]):
        own[j] = keep[j, y] + got[j, y]
        other[j] = (keep[j, 1 - y] + got[j, 1 - y]).astype(BF16)


def side_sum_body(rows, own, got, mine, s1, s2, s3):
    z = place()[0]
    planes, each = own.shape[:2]
    half = each - rows
    a_part = pl.ds(0, rows)
    for step, out in enumerate((mine, s1, s2, s3)):
        to = lax.rem(z + step, planes)
        piece = own[to, a_part, :] + got[to, a_part, :].astype(F32)
        out[pl.ds(0, rows), :] = piece.astype(out.dtype)
    for j in range(planes):
        piece = own[j, pl.ds(rows, half), :] + got[j, pl.ds(rows, half), :].astype(F32)
        piece = piece.astype(BF16)
        for out in (mine, s1, s2, s3):
            out[pl.ds(rows + j * half, half), :] = piece.astype(out.dtype)


def line_sum_body(mine, r1, r2, r3, grad_a, quarter):
    rows = grad_a.shape[0]
    total = (mine[...] + r2[...].astype(F32)) + (r1[...].astype(F32) + r3[...].astype(F32))
    grad_a[...] = total[:rows]
    quarter[...] = 2.0 * total[rows:]


def place_b_body(mine, side, core, core_side, out):
    _, y, c, _ = place()
    ranks = out.shape[0]
    half = ranks // 2
    planes = mine.shape[0] // half
    for ref, yy, cc in ((mine, y, c), (side, 1 - y, c), (core, y, 1 - c), (core_side, 1 - y, 1 - c)):
        row = pl.multiple_of(cc * half, half)
        for j in range(planes):
            column = pl.multiple_of((yy * planes + j) * ranks, ranks)
            out[pl.ds(row, half), pl.ds(column, ranks)] = ref[pl.ds(j * half, half), :]


def plane_body(k, first, rows, kept, counts, tok_far, cot, spread, down_far, *refs):
    pieces, refs = refs[: sum(counts)], refs[sum(counts) :]
    if first:
        shrink, up, act, acc, weight, block, tok, down, sem, sems = refs
    else:
        total, _, act, acc, weight, block, tok, down, sem, sems = refs
    z, y, c, x = place()
    depth = weight.shape[0]
    zz = lax.rem(z + 4 - k, 4)
    columns = pl.ds(pl.multiple_of(zz * depth, depth), depth)
    copies = fetch(((down_far.at[columns, :], down), (tok_far.at[:, columns], tok)), sems)
    middle = rows - 2 * kept

    def put(ref, at, count, to):
        weight[pl.ds(pl.multiple_of(to, STRIP), count), :] = ref[pl.ds(at, count), :]

    for h, cc in enumerate((c, 1 - c)):
        own = pieces[: counts[0]] if h == 0 else pieces[counts[0] :]
        where = []
        for ref in own:
            where += [(ref, at) for at in range(0, ref.shape[0], STRIP)]
        strips = iter(where)
        bases = [((y if i == 0 else 1 - y) * 2 + cc) * rows for i in range(2)]
        mine, inner, other = strip_places(cc, x)

        def next_strips(count, to):
            for i in range(count // STRIP):
                ref, at = next(strips, (None, 0))
                if ref is None:
                    here = pl.ds(pl.multiple_of(to + i * STRIP, STRIP), STRIP)
                    weight[here, :] = jnp.zeros((STRIP, weight.shape[1]), BF16)
                else:
                    put(ref, at, STRIP, to + i * STRIP)

        for base in bases:
            next_strips(kept, base + mine)
            next_strips(middle, base + inner)
        for base in bases:
            next_strips(kept, base + other)

    back = reduce_over_rows(cot[...], weight[...])
    copies[0].wait()
    back += reduce_over_rows(spread[...], down[...])
    block[...] = back.astype(BF16)
    copy = pltpu.make_async_copy(block, act.at[:, columns], sem)
    copy.start()
    copies[1].wait()
    forward = jnp.dot(tok[...], weight[...], preferred_element_type=F32)
    if first:
        forward += 2.0 * jnp.dot(shrink[...], up[...], preferred_element_type=F32)
    else:
        forward += total[...]
    acc[...] = forward
    copy.wait()


def last_body(k, rows, tok_far, cot, spread, down_far, own, got, total, _, act, values, *refs):
    tok, down, block, sems, sent = refs
    z, y, c, x = place()
    kept = own.shape[0]
    zz = lax.rem(z + 4 - k, 4)
    parts = []
    for cc in (c, 1 - c):
        start = ((zz * 2 + 1 - y) * 2 + cc) * rows + strip_places(cc, x)[2]
        parts.append(pl.ds(pl.multiple_of(start, BLOCK), kept))
    pairs = []
    for i, part in enumerate(parts):
        pairs += [(down_far.at[part, :], down.at[i]), (tok_far.at[:, part], tok.at[i])]
    copies = fetch(pairs, sems)
    outs = []
    for i, (part, weight) in enumerate(zip(parts, (own, got))):
        back = reduce_over_rows(cot[...], weight[...])
        copies[2 * i].wait()
        back += reduce_over_rows(spread[...], down[i])
        block[i] = back.astype(BF16)
        out = pltpu.make_async_copy(block.at[i], act.at[:, part], sent.at[i])
        out.start()
        outs.append(out)
    copies[1].wait()
    forward = total[...] + jnp.dot(tok[0], own[...], preferred_element_type=F32)
    copies[3].wait()
    forward += jnp.dot(tok[1], got[...], preferred_element_type=F32)
    values[...] = forward.astype(BF16)
    for out in outs:
        out.wait()


def cut_body(ref, out):
    out[...] = ref[pl.ds(0, out.shape[0]), :]


def pack_body(*refs):
    out, at = refs[-1], 0
    for ref in refs[:-1]:
        out[pl.ds(at, ref.shape[0]), :] = ref[...]
        at += ref.shape[0]


def swap(n, move):
    pairs = []
    for s in range(n):
        z, y, c = move(s // 4, s // 2 % 2, s % 2)
        pairs.append((s, (z % (n // 4) * 2 + y) * 2 + c))
    return pairs


def block_path(tokens, token_adapter_index, frozen, scales, down, up, cotangent):
    n, planes = 16, 4
    count, width = tokens.shape
    rows, columns = frozen.shape
    ranks = up.shape[0]
    depth = width // planes
    kept = 2 * STRIP
    shared_rows = rows - kept
    half = ranks // 2
    each = rows + half

    def over_z(name, v, by=1):
        with jax.named_scope(name):
            return lax.ppermute(v, "seq", swap(n, lambda z, y, c: (z + by, y, c)))

    def over_y(name, v):
        with jax.named_scope(name):
            return lax.ppermute(v, "seq", swap(n, lambda z, y, c: (z, 1 - y, c)))

    def over_core(name, v):
        with jax.named_scope(name):
            return lax.ppermute(v, "seq", swap(n, lambda z, y, c: (z, y, 1 - c)))

    def over_x(name, v):
        with jax.named_scope(name):
            return lax.ppermute(v, "groups", [(0, 1), (1, 0)])

    p0, rest = kernel(
        dequant_body,
        "scale_rows",
        5,
        [struct((shared_rows, columns), BF16), struct((kept, columns), BF16)],
        [HBM, HBM],
        [VMEM, VMEM],
        (frozen, scales.T),
        scratch=[
            pltpu.VMEM((rows, columns), BF16),
            pltpu.SMEM(scales.shape[::-1], F32),
            pltpu.SemaphoreType.DMA((2,)),
        ],
    )
    z1, y0 = over_z("z1", p0), over_y("y0", p0)

    piece = (planes, 2, each, ranks)
    shrink, spread, send, keep = kernel(
        functools.partial(grads_body, rows),
        "gradient_shares",
        6,
        [struct((count, ranks), BF16)] * 2 + [struct(piece, F32)] * 2,
        [HBM, VMEM, HBM, HBM, HBM, ANY],
        [VMEM] * 4,
        (tokens, token_adapter_index[None, :], down, up, cotangent, p0),
        scratch=[
            pltpu.VMEM(tokens.shape, BF16),
            pltpu.VMEM(down.shape, BF16),
            pltpu.VMEM(up.shape, BF16),
            pltpu.VMEM(cotangent.shape, BF16),
            pltpu.VMEM((count, ranks), F32),
            pltpu.SemaphoreType.DMA((2 + 2 * planes,)),
        ],
    )

    def plane(k, own, got, state):
        first = k == 0
        operands = [tokens, cotangent, spread, down] + own + got
        if first:
            operands += [shrink, up]
            specs = [HBM, VMEM, VMEM, HBM] + [VMEM] * (len(operands) - 4)
            alias = None
        else:
            operands += [state[1], state[0]]
            specs = [HBM, VMEM, VMEM, HBM] + [VMEM] * (len(operands) - 5) + [HBM]
            alias = {len(operands) - 1: 0}
        return kernel(
            functools.partial(plane_body, k, first, rows, kept, (len(own), len(got))),
            f"plane_{k}",
            GAP,
            [struct((count, width), BF16), struct((count, columns), F32)],
            specs,
            [HBM, VMEM],
            operands,
            scratch=[
                pltpu.VMEM((depth, columns), BF16),
                pltpu.VMEM((count, depth), BF16),
                pltpu.VMEM((count, depth), BF16),
                pltpu.VMEM((depth, ranks), BF16),
                pltpu.SemaphoreType.DMA,
                pltpu.SemaphoreType.DMA((2,)),
            ],
            alias=alias,
        )

    def pack(name, *parts):
        return kernel(
            pack_body,
            name,
            0,
            struct((sum(v.shape[0] for v in parts), columns), BF16),
            [VMEM] * len(parts),
            VMEM,
            parts,
        )

    def pack(name, *parts):
        return kernel(
            pack_body,
            name,
            0,
            struct((sum(v.shape[0] for v in parts), columns), BF16),
            [VMEM] * len(parts),
            VMEM,
            parts,
        )

    def last_rows(k, own, got, act, total):
        return kernel(
            functools.partial(last_body, k, rows),
            "last_rows",
            0,
            [struct((count, width), BF16), struct((count, columns), BF16)],
            [HBM, VMEM, VMEM, HBM, VMEM, VMEM, VMEM, HBM],
            [HBM, VMEM],
            [tokens, cotangent, spread, down, own, got, total, act],
            scratch=[
                pltpu.VMEM((2, count, kept), BF16),
                pltpu.VMEM((2, kept, ranks), BF16),
                pltpu.VMEM((2, count, kept), BF16),
                pltpu.SemaphoreType.DMA((4,)),
                pltpu.SemaphoreType.DMA((2,)),
            ],
            alias={7: 0},
        )

    e = {}
    last = []

    def event(*names):
        for name in names:
            if last and last[0] != name:
                e[name], e[last[0]] = lax.optimization_barrier((e[name], e[last[0]]))
            last[:] = [name]

    def cut(name, v, us=0.0):
        return kernel(
            cut_body, name, us, struct((kept, columns), BF16), [VMEM], VMEM, (v,)
        )

    def run_plane(k, own, got, state):
        own = [e[v] if isinstance(v, str) else v for v in own]
        state = plane(k, own, [e[v] for v in got], state)
        e["acc"] = state[1]
        event("acc")
        return state[0]

    e["share"] = over_core("core_share", send)
    e["z1"], e["y0"] = z1, y0
    event("z1")
    e["z2"], e["y1"] = over_z("z2", e["z1"]), over_y("y1", e["z1"])
    event("y0")
    e["x0"] = over_x("x0", e["y0"][:kept])
    e["cut"] = cut("cut_1", e["z1"], GAP)
    event("cut")
    e["x1a"] = over_x("x1a", e["cut"])
    event("share")
    e["own_y"], other_y = kernel(
        core_sum_body,
        "core_sum",
        0,
        [struct((planes, each, ranks), F32), struct((planes, each, ranks), BF16)],
        [VMEM] * 2,
        [VMEM] * 2,
        (keep, e["share"]),
    )
    event("own_y")
    e["side"] = over_y("side_share", other_y)
    event("z2")
    e["z3"], e["y2"] = over_z("z3", e["z2"]), over_y("y2", e["z2"])
    e["x2a"] = over_x("x2a", e["z2"][:kept])
    event("x1a")
    event("x0")
    e["c0"] = over_core("c0", pack("pack_0", p0, e["y0"], rest, e["x0"]))
    event("y1")
    e["x1b"] = over_x("x1b", e["y1"][:kept])
    event("side")
    line = struct((rows + planes * half, ranks), BF16)
    e["mine"], s1, s2, s3 = kernel(
        functools.partial(side_sum_body, rows),
        "side_sum",
        GAP,
        [struct(line.shape, F32), line, line, line],
        [VMEM] * 2,
        [VMEM] * 4,
        (e["own_y"], e["side"]),
    )
    event("mine")
    for i, v in enumerate((s1, s2, s3)):
        e[f"r{i + 1}"] = over_z(f"line_{i + 1}", v, i + 1)
    event("z3")
    e["y3"], e["x3a"] = over_y("y3", e["z3"]), over_x("x3a", e["z3"][:kept])
    event("x2a")
    event("x1b")
    e["c1"] = over_core("c1", pack("pack_1", e["z1"], e["y1"], e["x1a"], e["x1b"]))
    event("c0")
    act = run_plane(0, [p0, "y0", rest, "x0"], ["c0"], None)
    event("y2")
    e["x2b"] = over_x("x2b", e["y2"][:kept])
    event("x3a")
    event("c1")
    act = run_plane(1, ["z1", "y1", "x1a", "x1b"], ["c1"], (act, e["acc"]))
    event("y3")
    e["x3b"] = over_x("x3b", e["y3"][:kept])
    e["c3a"] = over_core("c3a", pack("pack_3", e["z3"], e["y3"], e["x3a"]))
    event("x2b")
    e["c2"] = over_core("c2", pack("pack_2", e["z2"], e["y2"], e["x2a"], e["x2b"]))
    event("r1")
    event("r2")
    event("r3")
    grad_a, e["quarter"] = kernel(
        line_sum_body,
        "line_sum",
        GAP,
        [struct((rows, ranks), F32), struct((planes * half, ranks), F32)],
        [VMEM] * 4,
        [VMEM] * 2,
        (e["mine"], e["r1"], e["r2"], e["r3"]),
    )
    event("quarter")
    e["side_quarter"] = over_y("side_up", e["quarter"])
    e["core_quarter"] = over_core("core_up", e["quarter"])
    event("c2")
    act = run_plane(2, ["z2", "y2", "x2a", "x2b"], ["c2"], (act, e["acc"]))
    event("c3a")
    act = run_plane(3, ["z3", "y3", "x3a"], ["c3a"], (act, e["acc"]))
    event("side_quarter")
    e["core_side"] = over_core("core_side_up", e["side_quarter"])
    event("core_quarter")
    event("core_side")
    grad_b = kernel(
        place_b_body,
        "place_up_gradient",
        0,
        struct((ranks, columns), F32),
        [VMEM] * 4,
        VMEM,
        (e["quarter"], e["side_quarter"], e["core_quarter"], e["core_side"]),
    )
    event("x3b")
    e["c3b"] = over_core("c3b", e["x3b"])
    event("c3b")
    act, values = last_rows(3, e["x3b"], e["c3b"], act, e["acc"])
    return values, act, grad_a, grad_b


def solution(mesh):
    sizes = (mesh.shape["groups"], mesh.shape["seq"])

    def on_device(*operands):
        rows, columns = operands[2].shape
        ranks = operands[5].shape[0]
        fits = rows == 5 * STRIP and columns == 8 * ranks
        path = block_path if sizes == (2, 16) and fits and ranks == BLOCK else plain_path
        return path(*operands)

    return jax.shard_map(
        on_device,
        mesh=mesh,
        in_specs=(
            P(("groups", "seq"), None),
            P(("groups", "seq")),
            P("seq", None),
            P(),
            P("groups", None),
            P("groups", None),
            P(("groups", "seq"), None),
        ),
        out_specs=(
            P(("groups", "seq"), None),
            P(("groups", "seq"), None),
            P(("groups", "seq"), None),
            P("groups", None),
        ),
        check_vma=False,
    )
```

```python
import functools

import jax
import jax.numpy as jnp
from jax import lax
from jax.experimental import pallas as pl
from jax.experimental.pallas import tpu as pltpu
from jax.sharding import PartitionSpec as P

BLOCK = 128
ADAPTER_RANK = 16
STRIP = 64
VMEM_LIMIT = 12 * 1024 * 1024
F32 = jnp.float32
BF16 = jnp.bfloat16


def dequant_rows(piece, scales):
    count = piece.shape[0]
    block_of = lax.iota(jnp.int32, count) // BLOCK
    select = (block_of[:, None] == lax.iota(jnp.int32, scales.shape[0])[None, :]).astype(F32)
    row_scales = jnp.dot(select, scales, precision=lax.Precision.HIGHEST)
    expanded = jnp.repeat(row_scales, BLOCK, axis=1)
    return (piece.astype(F32) * expanded).astype(BF16)


def reduce_over_rows(left, right):
    return lax.dot_general(left, right, (((1,), (1,)), ((), ())), preferred_element_type=F32)


def contract_tokens(left, right):
    return lax.dot_general(left, right, (((0,), (0,)), ((), ())), preferred_element_type=F32)


def plain_path(tokens, token_adapter_index, frozen, scales, down, up, cotangent):
    rank_adapter = lax.iota(jnp.int32, down.shape[1]) // ADAPTER_RANK
    mask = (token_adapter_index[:, None] == rank_adapter[None, :]).astype(F32)
    shrink = (jnp.dot(tokens, down, preferred_element_type=F32) * mask).astype(BF16)
    spread = (2.0 * reduce_over_rows(cotangent, up) * mask).astype(BF16)
    weight = dequant_rows(lax.all_gather(frozen, "seq", axis=0, tiled=True), scales)
    values = jnp.dot(tokens, weight, preferred_element_type=F32)
    values = (values + 2.0 * jnp.dot(shrink, up, preferred_element_type=F32)).astype(BF16)
    act = reduce_over_rows(cotangent, weight) + reduce_over_rows(spread, down)
    grad_a = lax.psum_scatter(
        contract_tokens(tokens, spread), "seq", scatter_dimension=0, tiled=True
    )
    grad_b = lax.psum(2.0 * contract_tokens(shrink, cotangent), "seq")
    return values, act.astype(BF16), grad_a, grad_b


GAPS = {'plane_1': 0, 'pack_1': 60, 'place_up_gradient': 2, 'side_sum': 5, 'pack_0': 0, 'line_sum': 0}
GAP = 60
VMEM = pl.BlockSpec(memory_space=pltpu.VMEM)
SMEM = pl.BlockSpec(memory_space=pltpu.SMEM)
ANY = pl.BlockSpec(memory_space=pl.ANY)
HBM = pl.BlockSpec(memory_space=pltpu.HBM)


def struct(shape, dtype):
    return jax.ShapeDtypeStruct(shape, dtype)


def kernel(body, name, us, out_shape, in_specs, out_specs, operands, scratch=(), alias=None):
    return pl.pallas_call(
        body,
        name=name,
        in_specs=in_specs,
        out_specs=out_specs,
        out_shape=out_shape,
        scratch_shapes=scratch,
        input_output_aliases=alias or {},
        compiler_params=pltpu.CompilerParams(vmem_limit_bytes=VMEM_LIMIT),
        cost_estimate=pl.CostEstimate(
            flops=int(GAPS.get(name, us) * 1.1e9), bytes_accessed=1, transcendentals=0
        ),
    )(*operands)


def after(value, *others):
    return lax.optimization_barrier((value,) + others)[0]


def place():
    s = lax.axis_index("seq")
    return s // 4, s // 2 % 2, s % 2, lax.axis_index("groups")


def strip_places(core, x):
    low = core * STRIP
    return low + x * (2 * STRIP), (1 - core) * (4 * STRIP), low + (1 - x) * (2 * STRIP)


def fetch(pairs, sems):
    copies = [pltpu.make_async_copy(a, b, sems.at[i]) for i, (a, b) in enumerate(pairs)]
    for copy in copies:
        copy.start()
    return copies


def dequant_body(w_far, scales_far, shared, rest, w, scales, sems):
    for copy in fetch(((scales_far, scales), (w_far, w)), sems):
        copy.wait()
    z, y, c, x = place()
    first = ((z * 2 + y) * 2 + c) * (w.shape[0] // STRIP)

    def scale_strips(out, at, count, source):
        for i in range(count // STRIP):
            start = source + i * STRIP
            block_row = (first * STRIP + start) // BLOCK
            rows = pl.ds(pl.multiple_of(start, STRIP), STRIP)
            for b in range(w.shape[1] // BLOCK):
                columns = pl.ds(b * BLOCK, BLOCK)
                value = w[rows, columns].astype(F32) * scales[b, block_row]
                out[pl.ds(at + i * STRIP, STRIP), columns] = value.astype(BF16)

    kept = rest.shape[0]
    mine, middle, other = strip_places(c, x)
    scale_strips(shared, 0, kept, mine)
    scale_strips(shared, kept, shared.shape[0] - kept, middle)
    scale_strips(rest, 0, kept, other)


def grads_body(rows, tok_far, idx, down_far, up_far, cot_far, _, *refs):
    shrink, spread, send, keep, tok, down, up, cot, acc, sems = refs
    c = place()[2]
    ranks, planes = up.shape[0], send.shape[0]
    depth = tok.shape[1] // planes
    half = ranks // 2
    pairs = [(up_far, up), (cot_far, cot)]
    for j in range(planes):
        part = pl.ds(j * depth, depth)
        pairs += [(tok_far.at[:, part], tok.at[:, part]), (down_far.at[part, :], down.at[part, :])]
    copies = fetch(pairs, sems)
    rank_adapter = lax.broadcasted_iota(jnp.int32, (ranks, 1), 0) // ADAPTER_RANK
    mask = (idx[...] == rank_adapter).astype(F32).T
    copies[0].wait()
    copies[1].wait()
    spread[...] = (2.0 * reduce_over_rows(cot[...], up[...]) * mask).astype(BF16)

    def store(j, y, core, at, value):
        @pl.when(c == core)
        def _():
            keep[j, y, pl.ds(at, value.shape[0]), :] = value

        @pl.when(c != core)
        def _():
            send[j, y, pl.ds(at, value.shape[0]), :] = value

    for j in range(planes):
        copies[2 + 2 * j].wait()
        copies[3 + 2 * j].wait()
        block = tok[:, j * depth : (j + 1) * depth]
        sum_j = jnp.dot(block, down[j * depth : (j + 1) * depth], preferred_element_type=F32)
        if j == 0:
            acc[...] = sum_j
        else:
            acc[...] += sum_j
        part = contract_tokens(block, spread[...])
        for y in range(2):
            for core in range(2):
                at = (y * 2 + core) * rows
                store(j, y, core, 0, part[at : at + rows])
    shrink[...] = (acc[...] * mask).astype(BF16)
    grad_b = contract_tokens(shrink[...], cot[...])
    for y in range(2):
        for j in range(planes):
            at = (y * planes + j) * ranks
            for core in range(2):
                piece = grad_b[core * half : (core + 1) * half, at : at + ranks]
                store(j, y, core, rows, piece)


def core_sum_body(keep, got, own, other):
    y = place()[1]
    for j in range(keep.shape[0]):
        own[j] = keep[j, y] + got[j, y]
        other[j] = (keep[j, 1 - y] + got[j, 1 - y]).astype(BF16)


def side_sum_body(rows, own, got, mine, s1, s2, s3):
    z = place()[0]
    planes, each = own.shape[:2]
    half = each - rows
    a_part = pl.ds(0, rows)
    for step, out in enumerate((mine, s1, s2, s3)):
        to = lax.rem(z + step, planes)
        piece = own[to, a_part, :] + got[to, a_part, :].astype(F32)
        out[pl.ds(0, rows), :] = piece.astype(out.dtype)
    for j in range(planes):
        piece = own[j, pl.ds(rows, half), :] + got[j, pl.ds(rows, half), :].astype(F32)
        piece = piece.astype(BF16)
        for out in (mine, s1, s2, s3):
            out[pl.ds(rows + j * half, half), :] = piece.astype(out.dtype)


def line_sum_body(mine, r1, r2, r3, grad_a, quarter):
    rows = grad_a.shape[0]
    total = (mine[...] + r2[...].astype(F32)) + (r1[...].astype(F32) + r3[...].astype(F32))
    grad_a[...] = total[:rows]
    quarter[...] = 2.0 * total[rows:]


def place_b_body(mine, core, out):
    _, y, c, _ = place()
    ranks = out.shape[0]
    half = ranks // 2
    planes = mine.shape[0] // (2 * half)
    for ref, cc in ((mine, c), (core, 1 - c)):
        row = pl.multiple_of(cc * half, half)
        for j in range(2 * planes):
            yy = y if j < planes else 1 - y
            column = pl.multiple_of((yy * planes + j % planes) * ranks, ranks)
            out[pl.ds(row, half), pl.ds(column, ranks)] = ref[pl.ds(j * half, half), :]


def plane_body(k, first, rows, kept, counts, tok_far, cot, spread, down_far, *refs):
    pieces, refs = refs[: sum(counts)], refs[sum(counts) :]
    if first:
        shrink, up, act, acc, *saved, weight, block, tok, down, sem, sems = refs
    else:
        total, _, act, acc, *saved, weight, block, tok, down, sem, sems = refs
    z, y, c, x = place()
    depth = weight.shape[0]
    zz = lax.rem(z + 4 - k, 4)
    columns = pl.ds(pl.multiple_of(zz * depth, depth), depth)
    copies = fetch(((down_far.at[columns, :], down), (tok_far.at[:, columns], tok)), sems)
    middle = rows - 2 * kept

    def put(ref, at, count, to):
        weight[pl.ds(pl.multiple_of(to, STRIP), count), :] = ref[pl.ds(at, count), :]

    for h, cc in enumerate((c, 1 - c)):
        own = pieces[: counts[0]] if h == 0 else pieces[counts[0] :]
        where = []
        for ref in own:
            where += [(ref, at) for at in range(0, ref.shape[0], STRIP)]
        strips = iter(where)
        bases = [((y if i == 0 else 1 - y) * 2 + cc) * rows for i in range(2)]
        mine, inner, other = strip_places(cc, x)

        def next_strips(count, to):
            for i in range(count // STRIP):
                ref, at = next(strips, (None, 0))
                if ref is None:
                    here = pl.ds(pl.multiple_of(to + i * STRIP, STRIP), STRIP)
                    weight[here, :] = jnp.zeros((STRIP, weight.shape[1]), BF16)
                else:
                    put(ref, at, STRIP, to + i * STRIP)

        for base in bases:
            next_strips(kept, base + mine)
            next_strips(middle, base + inner)
        for base in bases:
            next_strips(kept, base + other)

    back = reduce_over_rows(cot[...], weight[...])
    copies[0].wait()
    back += reduce_over_rows(spread[...], down[...])
    block[...] = back.astype(BF16)
    copy = pltpu.make_async_copy(block, act.at[:, columns], sem)
    copy.start()
    copies[1].wait()
    forward = jnp.dot(tok[...], weight[...], preferred_element_type=F32)
    if first:
        forward += 2.0 * jnp.dot(shrink[...], up[...], preferred_element_type=F32)
    else:
        forward += total[...]
    acc[...] = forward
    if saved:
        for i in range(2):
            here = pl.ds(late_rows(k, rows, i, x, z, y, c)[0], kept)
            saved[0][i] = tok[:, here]
            saved[1][i] = down[here, :]
    copy.wait()


def late_rows(k, rows, i, x, z, y, c):
    cc = c if i == 0 else 1 - c
    within = ((1 - y) * 2 + cc) * rows + strip_places(cc, x)[2]
    zz = lax.rem(z + 4 - k, 4)
    return pl.multiple_of(within, BLOCK), pl.multiple_of(zz * 4 * rows + within, BLOCK)


def last_body(k, rows, i, tok, cot, spread, down, weight, total, _, act, out, block, sem):
    z, y, c, x = place()
    kept = weight.shape[0]
    start = late_rows(k, rows, i, x, z, y, c)[1]
    back = reduce_over_rows(cot[...], weight[...])
    back += reduce_over_rows(spread[...], down[i])
    block[...] = back.astype(BF16)
    copy = pltpu.make_async_copy(block, act.at[:, pl.ds(start, kept)], sem)
    copy.start()
    forward = total[...] + jnp.dot(tok[i], weight[...], preferred_element_type=F32)
    out[...] = forward.astype(out.dtype)
    copy.wait()


def cut_body(ref, out):
    out[...] = ref[pl.ds(0, out.shape[0]), :]


def pack_body(*refs):
    out, at = refs[-1], 0
    for ref in refs[:-1]:
        out[pl.ds(at, ref.shape[0]), :] = ref[...]
        at += ref.shape[0]


def swap(n, move):
    pairs = []
    for s in range(n):
        z, y, c = move(s // 4, s // 2 % 2, s % 2)
        pairs.append((s, (z % (n // 4) * 2 + y) * 2 + c))
    return pairs


def block_path(tokens, token_adapter_index, frozen, scales, down, up, cotangent):
    n, planes = 16, 4
    count, width = tokens.shape
    rows, columns = frozen.shape
    ranks = up.shape[0]
    depth = width // planes
    kept = 2 * STRIP
    shared_rows = rows - kept
    half = ranks // 2
    each = rows + half

    def over_z(name, v, by=1):
        with jax.named_scope(name):
            return lax.ppermute(v, "seq", swap(n, lambda z, y, c: (z + by, y, c)))

    def over_y(name, v):
        with jax.named_scope(name):
            return lax.ppermute(v, "seq", swap(n, lambda z, y, c: (z, 1 - y, c)))

    def over_core(name, v):
        with jax.named_scope(name):
            return lax.ppermute(v, "seq", swap(n, lambda z, y, c: (z, y, 1 - c)))

    def over_x(name, v):
        with jax.named_scope(name):
            return lax.ppermute(v, "groups", [(0, 1), (1, 0)])

    p0, rest = kernel(
        dequant_body,
        "scale_rows",
        5,
        [struct((shared_rows, columns), BF16), struct((kept, columns), BF16)],
        [HBM, HBM],
        [VMEM, VMEM],
        (frozen, scales.T),
        scratch=[
            pltpu.VMEM((rows, columns), BF16),
            pltpu.SMEM(scales.shape[::-1], F32),
            pltpu.SemaphoreType.DMA((2,)),
        ],
    )
    z1, y0 = over_z("z1", p0), over_y("y0", p0)

    piece = (planes, 2, each, ranks)
    shrink, spread, send, keep = kernel(
        functools.partial(grads_body, rows),
        "gradient_shares",
        6,
        [struct((count, ranks), BF16)] * 2 + [struct(piece, F32)] * 2,
        [HBM, VMEM, HBM, HBM, HBM, ANY],
        [VMEM] * 4,
        (tokens, token_adapter_index[None, :], down, up, cotangent, p0),
        scratch=[
            pltpu.VMEM(tokens.shape, BF16),
            pltpu.VMEM(down.shape, BF16),
            pltpu.VMEM(up.shape, BF16),
            pltpu.VMEM(cotangent.shape, BF16),
            pltpu.VMEM((count, ranks), F32),
            pltpu.SemaphoreType.DMA((2 + 2 * planes,)),
        ],
    )

    def plane(k, own, got, state, us):
        first = k == 0
        kinds = []
        if k == planes - 1:
            kinds = [struct((2, count, kept), BF16), struct((2, kept, ranks), BF16)]
        operands = [tokens, cotangent, e["spread"], down] + own + got
        if first:
            operands += [shrink, up]
            specs = [HBM, VMEM, VMEM, HBM] + [VMEM] * (len(operands) - 4)
            alias = None
        else:
            operands += [state[1], state[0]]
            specs = [HBM, VMEM, VMEM, HBM] + [VMEM] * (len(operands) - 5) + [HBM]
            alias = {len(operands) - 1: 0}
        return kernel(
            functools.partial(plane_body, k, first, rows, kept, (len(own), len(got))),
            f"plane_{k}",
            us,
            [struct((count, width), BF16), struct((count, columns), F32)] + kinds,
            specs,
            [HBM, VMEM] + [VMEM] * len(kinds),
            operands,
            scratch=[
                pltpu.VMEM((depth, columns), BF16),
                pltpu.VMEM((count, depth), BF16),
                pltpu.VMEM((count, depth), BF16),
                pltpu.VMEM((depth, ranks), BF16),
                pltpu.SemaphoreType.DMA,
                pltpu.SemaphoreType.DMA((2,)),
            ],
            alias=alias,
        )

    def pack(name, *parts):
        return kernel(
            pack_body,
            name,
            GAP,
            struct((sum(v.shape[0] for v in parts), parts[0].shape[1]), parts[0].dtype),
            [VMEM] * len(parts),
            VMEM,
            parts,
        )

    def pack(name, *parts):
        return kernel(
            pack_body,
            name,
            GAP,
            struct((sum(v.shape[0] for v in parts), parts[0].shape[1]), parts[0].dtype),
            [VMEM] * len(parts),
            VMEM,
            parts,
        )

    def last_rows(k, i, weight, state, saved):
        return kernel(
            functools.partial(last_body, k, rows, i),
            f"last_rows_{i}",
            GAP,
            [struct((count, width), BF16), struct((count, columns), (F32, BF16)[i])],
            [VMEM] * 6 + [HBM],
            [HBM, VMEM],
            [saved[0], cotangent, e["spread"], saved[1], weight, state[1], state[0]],
            scratch=[pltpu.VMEM((count, kept), BF16), pltpu.SemaphoreType.DMA],
            alias={6: 0},
        )

    e = {"send": send, "spread": spread, "z1": z1, "y0": y0}

    def event(name):
        e[name], e["spread"] = lax.optimization_barrier((e[name], e["spread"]))

    def cut(name, v, us):
        return kernel(
            cut_body, name, us, struct((kept, columns), BF16), [VMEM], VMEM, (v,)
        )

    def run_plane(k, own, got):
        own = [e[v] if isinstance(v, str) else v for v in own]
        state = (e["act"], e["acc"]) if k else None
        e["act"], e["acc"], *e["saved"] = plane(k, own, [e[got]], state, GAP)

    def run_last(i, name):
        e["act"], e["acc"] = last_rows(3, i, e[name], (e["act"], e["acc"]), e["saved"])
        return e["acc"]

    e["core_share"] = over_core("core_share", e["send"])
    event("z1")
    e["z2"] = over_z("z2", e["z1"])
    e["y1"] = over_y("y1", e["z1"])
    event("z1")
    e["cut"] = cut("cut_1", e["z1"], GAP)
    event("cut")
    e["x1a"] = over_x("x1a", e["cut"])
    event("y0")
    e["x0"] = over_x("x0", e["y0"][:kept])
    event("core_share")
    event("x0")
    event("core_share")
    e["own_y"], e["other_y"] = kernel(
        core_sum_body,
        "core_sum",
        GAP,
        [struct((planes, each, ranks), F32), struct((planes, each, ranks), BF16)],
        [VMEM] * 2,
        [VMEM] * 2,
        (keep, e["core_share"]),
    )
    event("own_y")
    e["side_share"] = over_y("side_share", e["other_y"])
    event("y1")
    e["x1b"] = over_x("x1b", e["y1"][:kept])
    event("z2")
    e["z3"] = over_z("z3", e["z2"])
    e["y2"] = over_y("y2", e["z2"])
    e["x2a"] = over_x("x2a", e["z2"][:kept])
    event("x1a")
    event("x1b")
    event("x0")
    e["pack_0"] = pack("pack_0", p0, e["y0"], rest, e["x0"])
    event("pack_0")
    e["c0"] = over_core("c0", e["pack_0"])
    event("side_share")
    line = struct((rows + planes * half, ranks), BF16)
    e["mine"], e["s1"], e["s2"], e["s3"] = kernel(
        functools.partial(side_sum_body, rows),
        "side_sum",
        GAP,
        [struct(line.shape, F32), line, line, line],
        [VMEM] * 2,
        [VMEM] * 4,
        (e["own_y"], e["side_share"]),
    )
    event("mine")
    e["line_1"] = over_z("line_1", e["s1"], 1)
    e["line_2"] = over_z("line_2", e["s2"], 2)
    e["line_3"] = over_z("line_3", e["s3"], 3)
    event("x1b")
    e["pack_1"] = pack("pack_1", e["z1"], e["y1"], e["x1a"], e["x1b"])
    event("pack_1")
    e["c1"] = over_core("c1", e["pack_1"])
    event("z3")
    e["y3"] = over_y("y3", e["z3"])
    e["x3a"] = over_x("x3a", e["z3"][:kept])
    event("x2a")
    event("c0")
    event("y2")
    e["x2b"] = over_x("x2b", e["y2"][:kept])
    event("line_3")
    event("c0")
    run_plane(0, [p0, "y0", rest, "x0"], "c0")
    event("acc")
    event("c1")
    run_plane(1, ["z1", "y1", "x1a", "x1b"], "c1")
    event("acc")
    event("x3a")
    event("y3")
    e["x3b"] = over_x("x3b", e["y3"][:kept])
    event("x2b")
    e["pack_2"] = pack("pack_2", e["z2"], e["y2"], e["x2a"], e["x2b"])
    event("pack_2")
    e["c2"] = over_core("c2", e["pack_2"])
    event("line_2")
    event("x3a")
    e["pack_3"] = pack("pack_3", e["z3"], e["y3"], e["x3a"])
    event("pack_3")
    e["c3a"] = over_core("c3a", e["pack_3"])
    event("line_1")
    grad_a, e["quarter"] = kernel(
        line_sum_body,
        "line_sum",
        GAP,
        [struct((rows, ranks), F32), struct((planes * half, ranks), F32)],
        [VMEM] * 4,
        [VMEM] * 2,
        (e["mine"], e["line_1"], e["line_2"], e["line_3"]),
    )
    event("quarter")
    e["side_up"] = over_y("side_up", e["quarter"])
    event("c2")
    run_plane(2, ["z2", "y2", "x2a", "x2b"], "c2")
    event("acc")
    event("side_up")
    e["both"] = pack("pack_up", e["quarter"], e["side_up"])
    event("both")
    e["core_up"] = over_core("core_up", e["both"])
    event("c3a")
    run_plane(3, ["z3", "y3", "x3a"], "c3a")
    event("acc")
    event("core_up")
    event("x3b")
    e["c3b"] = over_core("c3b", e["x3b"])
    event("core_up")
    grad_b = kernel(
        place_b_body,
        "place_up_gradient",
        GAP,
        struct((ranks, columns), F32),
        [VMEM] * 2,
        VMEM,
        (e["both"], e["core_up"]),
    )
    event("x3b")
    run_last(0, "x3b")
    event("acc")
    event("c3b")
    values = run_last(1, "c3b")
    act, values = e["act"], e["acc"]
    return values, act, grad_a, grad_b


def solution(mesh):
    sizes = (mesh.shape["groups"], mesh.shape["seq"])

    def on_device(*operands):
        rows, columns = operands[2].shape
        ranks = operands[5].shape[0]
        fits = rows == 5 * STRIP and columns == 8 * ranks
        path = block_path if sizes == (2, 16) and fits and ranks == BLOCK else plain_path
        return path(*operands)

    return jax.shard_map(
        on_device,
        mesh=mesh,
        in_specs=(
            P(("groups", "seq"), None),
            P(("groups", "seq")),
            P("seq", None),
            P(),
            P("groups", None),
            P("groups", None),
            P(("groups", "seq"), None),
        ),
        out_specs=(
            P(("groups", "seq"), None),
            P(("groups", "seq"), None),
            P(("groups", "seq"), None),
            P("groups", None),
        ),
        check_vma=False,
    )
```

```python
import functools

import jax
import jax.numpy as jnp
from jax import lax
from jax.experimental import pallas as pl
from jax.experimental.pallas import tpu as pltpu
from jax.sharding import PartitionSpec as P

BLOCK = 128
ADAPTER_RANK = 16
STRIP = 64
VMEM_LIMIT = 12 * 1024 * 1024
STEP_US = 20
F32 = jnp.float32
BF16 = jnp.bfloat16


def dequant_rows(piece, scales):
    count = piece.shape[0]
    block_of = lax.iota(jnp.int32, count) // BLOCK
    select = (block_of[:, None] == lax.iota(jnp.int32, scales.shape[0])[None, :]).astype(F32)
    row_scales = jnp.dot(select, scales, precision=lax.Precision.HIGHEST)
    expanded = jnp.repeat(row_scales, BLOCK, axis=1)
    return (piece.astype(F32) * expanded).astype(BF16)


def reduce_over_rows(left, right):
    return lax.dot_general(left, right, (((1,), (1,)), ((), ())), preferred_element_type=F32)


def contract_tokens(left, right):
    return lax.dot_general(left, right, (((0,), (0,)), ((), ())), preferred_element_type=F32)


def plain_path(tokens, token_adapter_index, frozen, scales, down, up, cotangent):
    rank_adapter = lax.iota(jnp.int32, down.shape[1]) // ADAPTER_RANK
    mask = (token_adapter_index[:, None] == rank_adapter[None, :]).astype(F32)
    shrink = (jnp.dot(tokens, down, preferred_element_type=F32) * mask).astype(BF16)
    spread = (2.0 * reduce_over_rows(cotangent, up) * mask).astype(BF16)
    weight = dequant_rows(lax.all_gather(frozen, "seq", axis=0, tiled=True), scales)
    values = jnp.dot(tokens, weight, preferred_element_type=F32)
    values = (values + 2.0 * jnp.dot(shrink, up, preferred_element_type=F32)).astype(BF16)
    act = reduce_over_rows(cotangent, weight) + reduce_over_rows(spread, down)
    grad_a = lax.psum_scatter(
        contract_tokens(tokens, spread), "seq", scatter_dimension=0, tiled=True
    )
    grad_b = lax.psum(2.0 * contract_tokens(shrink, cotangent), "seq")
    return values, act.astype(BF16), grad_a, grad_b


OTHER_US = dict(plane_1=0, place_up_gradient=2, side_sum=5, pack_0=0, line_sum=0, pack_2=2, pack_up=2, scale_rows=5, gradient_shares=6)
VMEM = pl.BlockSpec(memory_space=pltpu.VMEM)
SMEM = pl.BlockSpec(memory_space=pltpu.SMEM)
ANY = pl.BlockSpec(memory_space=pl.ANY)
HBM = pl.BlockSpec(memory_space=pltpu.HBM)


def struct(shape, dtype):
    return jax.ShapeDtypeStruct(shape, dtype)


def kernel(body, name, out_shape, in_specs, out_specs, operands, scratch=(), alias=None):
    return pl.pallas_call(
        body,
        name=name,
        in_specs=in_specs,
        out_specs=out_specs,
        out_shape=out_shape,
        scratch_shapes=scratch,
        input_output_aliases=alias or {},
        compiler_params=pltpu.CompilerParams(vmem_limit_bytes=VMEM_LIMIT),
        cost_estimate=pl.CostEstimate(
            flops=int(OTHER_US.get(name, STEP_US) * 1.1e9), bytes_accessed=1, transcendentals=0
        ),
    )(*operands)


def hold(value, after):
    return lax.optimization_barrier((value, after))


def place():
    s = lax.axis_index("seq")
    return s // 4, s // 2 % 2, s % 2, lax.axis_index("groups")


def strip_places(core, x):
    low = core * STRIP
    return low + x * (2 * STRIP), (1 - core) * (4 * STRIP), low + (1 - x) * (2 * STRIP)


def fetch(pairs, sems):
    copies = [pltpu.make_async_copy(a, b, sems.at[i]) for i, (a, b) in enumerate(pairs)]
    for copy in copies:
        copy.start()
    return copies


def dequant_body(w_far, scales_far, shared, rest, w, scales, sems):
    for copy in fetch(((scales_far, scales), (w_far, w)), sems):
        copy.wait()
    z, y, c, x = place()
    first = ((z * 2 + y) * 2 + c) * (w.shape[0] // STRIP)

    def scale_strips(out, at, count, source):
        for i in range(count // STRIP):
            start = source + i * STRIP
            block_row = (first * STRIP + start) // BLOCK
            rows = pl.ds(pl.multiple_of(start, STRIP), STRIP)
            for b in range(w.shape[1] // BLOCK):
                columns = pl.ds(b * BLOCK, BLOCK)
                value = w[rows, columns].astype(F32) * scales[b, block_row]
                out[pl.ds(at + i * STRIP, STRIP), columns] = value.astype(BF16)

    kept = rest.shape[0]
    mine, middle, other = strip_places(c, x)
    scale_strips(shared, 0, kept, mine)
    scale_strips(shared, kept, shared.shape[0] - kept, middle)
    scale_strips(rest, 0, kept, other)


def grads_body(rows, tok_far, idx, down_far, up_far, cot_far, _, *refs):
    shrink, spread, send, keep, tok, down, up, cot, acc, sems = refs
    c = place()[2]
    ranks, planes = up.shape[0], send.shape[0]
    depth = tok.shape[1] // planes
    half = ranks // 2
    pairs = [(up_far, up), (cot_far, cot)]
    for j in range(planes):
        part = pl.ds(j * depth, depth)
        pairs += [(tok_far.at[:, part], tok.at[:, part]), (down_far.at[part, :], down.at[part, :])]
    copies = fetch(pairs, sems)
    rank_adapter = lax.broadcasted_iota(jnp.int32, (ranks, 1), 0) // ADAPTER_RANK
    mask = (idx[...] == rank_adapter).astype(F32).T
    copies[0].wait()
    copies[1].wait()
    spread[...] = (2.0 * reduce_over_rows(cot[...], up[...]) * mask).astype(BF16)

    def store(j, y, core, at, value):
        @pl.when(c == core)
        def _():
            keep[j, y, pl.ds(at, value.shape[0]), :] = value

        @pl.when(c != core)
        def _():
            send[j, y, pl.ds(at, value.shape[0]), :] = value

    for j in range(planes):
        copies[2 + 2 * j].wait()
        copies[3 + 2 * j].wait()
        block = tok[:, j * depth : (j + 1) * depth]
        sum_j = jnp.dot(block, down[j * depth : (j + 1) * depth], preferred_element_type=F32)
        if j == 0:
            acc[...] = sum_j
        else:
            acc[...] += sum_j
        part = contract_tokens(block, spread[...])
        for y in range(2):
            for core in range(2):
                at = (y * 2 + core) * rows
                store(j, y, core, 0, part[at : at + rows])
    shrink[...] = (acc[...] * mask).astype(BF16)
    grad_b = contract_tokens(shrink[...], cot[...])
    for y in range(2):
        for j in range(planes):
            at = (y * planes + j) * ranks
            for core in range(2):
                piece = grad_b[core * half : (core + 1) * half, at : at + ranks]
                store(j, y, core, rows, piece)


def core_sum_body(keep, got, own, other):
    y = place()[1]
    for j in range(keep.shape[0]):
        own[j] = keep[j, y] + got[j, y]
        other[j] = (keep[j, 1 - y] + got[j, 1 - y]).astype(BF16)


def side_sum_body(rows, own, got, mine, s1, s2, s3):
    z = place()[0]
    planes, each = own.shape[:2]
    half = each - rows
    a_part = pl.ds(0, rows)
    for step, out in enumerate((mine, s1, s2, s3)):
        to = lax.rem(z + step, planes)
        piece = own[to, a_part, :] + got[to, a_part, :].astype(F32)
        out[pl.ds(0, rows), :] = piece.astype(out.dtype)
    for j in range(planes):
        piece = own[j, pl.ds(rows, half), :] + got[j, pl.ds(rows, half), :].astype(F32)
        piece = piece.astype(BF16)
        for out in (mine, s1, s2, s3):
            out[pl.ds(rows + j * half, half), :] = piece.astype(out.dtype)


def line_sum_body(mine, r1, r2, r3, grad_a, quarter):
    rows = grad_a.shape[0]
    total = (mine[...] + r2[...].astype(F32)) + (r1[...].astype(F32) + r3[...].astype(F32))
    grad_a[...] = total[:rows]
    quarter[...] = 2.0 * total[rows:]


def place_b_body(mine, core, out):
    _, y, c, _ = place()
    ranks = out.shape[0]
    half = ranks // 2
    planes = mine.shape[0] // (2 * half)
    for ref, cc in ((mine, c), (core, 1 - c)):
        row = pl.multiple_of(cc * half, half)
        for j in range(2 * planes):
            yy = y if j < planes else 1 - y
            column = pl.multiple_of((yy * planes + j % planes) * ranks, ranks)
            out[pl.ds(row, half), pl.ds(column, ranks)] = ref[pl.ds(j * half, half), :]


def plane_body(k, first, rows, kept, counts, tok_far, cot, spread, down_far, *refs):
    pieces, refs = refs[: sum(counts)], refs[sum(counts) :]
    if first:
        shrink, up, act, acc, *saved, weight, block, tok, down, sem, sems = refs
    else:
        total, _, act, acc, *saved, weight, block, tok, down, sem, sems = refs
    z, y, c, x = place()
    depth = weight.shape[0]
    zz = lax.rem(z + 4 - k, 4)
    columns = pl.ds(pl.multiple_of(zz * depth, depth), depth)
    copies = fetch(((down_far.at[columns, :], down), (tok_far.at[:, columns], tok)), sems)
    middle = rows - 2 * kept

    def put(ref, at, count, to):
        weight[pl.ds(pl.multiple_of(to, STRIP), count), :] = ref[pl.ds(at, count), :]

    for h, cc in enumerate((c, 1 - c)):
        own = pieces[: counts[0]] if h == 0 else pieces[counts[0] :]
        where = []
        for ref in own:
            where += [(ref, at) for at in range(0, ref.shape[0], STRIP)]
        strips = iter(where)
        bases = [((y if i == 0 else 1 - y) * 2 + cc) * rows for i in range(2)]
        mine, inner, other = strip_places(cc, x)

        def next_strips(count, to):
            for i in range(count // STRIP):
                ref, at = next(strips, (None, 0))
                if ref is None:
                    here = pl.ds(pl.multiple_of(to + i * STRIP, STRIP), STRIP)
                    weight[here, :] = jnp.zeros((STRIP, weight.shape[1]), BF16)
                else:
                    put(ref, at, STRIP, to + i * STRIP)

        for base in bases:
            next_strips(kept, base + mine)
            next_strips(middle, base + inner)
        for base in bases:
            next_strips(kept, base + other)

    back = reduce_over_rows(cot[...], weight[...])
    copies[0].wait()
    back += reduce_over_rows(spread[...], down[...])
    block[...] = back.astype(BF16)
    copy = pltpu.make_async_copy(block, act.at[:, columns], sem)
    copy.start()
    copies[1].wait()
    forward = jnp.dot(tok[...], weight[...], preferred_element_type=F32)
    if first:
        forward += 2.0 * jnp.dot(shrink[...], up[...], preferred_element_type=F32)
    else:
        forward += total[...]
    acc[...] = forward
    if saved:
        for i in range(2):
            here = pl.ds(late_rows(k, rows, i, x, z, y, c)[0], kept)
            saved[0][i] = tok[:, here]
            saved[1][i] = down[here, :]
    copy.wait()


def late_rows(k, rows, i, x, z, y, c):
    cc = c if i == 0 else 1 - c
    within = ((1 - y) * 2 + cc) * rows + strip_places(cc, x)[2]
    zz = lax.rem(z + 4 - k, 4)
    return pl.multiple_of(within, BLOCK), pl.multiple_of(zz * 4 * rows + within, BLOCK)


def last_body(k, rows, i, tok, cot, spread, down, weight, total, _, act, out, block, sem):
    z, y, c, x = place()
    kept = weight.shape[0]
    start = late_rows(k, rows, i, x, z, y, c)[1]
    back = reduce_over_rows(cot[...], weight[...])
    back += reduce_over_rows(spread[...], down[i])
    block[...] = back.astype(BF16)
    copy = pltpu.make_async_copy(block, act.at[:, pl.ds(start, kept)], sem)
    copy.start()
    forward = total[...] + jnp.dot(tok[i], weight[...], preferred_element_type=F32)
    out[...] = forward.astype(out.dtype)
    copy.wait()


def cut_body(ref, out):
    out[...] = ref[pl.ds(0, out.shape[0]), :]


def pack_body(*refs):
    out, at = refs[-1], 0
    for ref in refs[:-1]:
        out[pl.ds(at, ref.shape[0]), :] = ref[...]
        at += ref.shape[0]


def swap(n, move):
    pairs = []
    for s in range(n):
        z, y, c = move(s // 4, s // 2 % 2, s % 2)
        pairs.append((s, (z % (n // 4) * 2 + y) * 2 + c))
    return pairs


def block_path(tokens, token_adapter_index, frozen, scales, down, up, cotangent):
    n, planes = 16, 4
    count, width = tokens.shape
    rows, columns = frozen.shape
    ranks = up.shape[0]
    depth = width // planes
    kept = 2 * STRIP
    shared_rows = rows - kept
    half = ranks // 2
    each = rows + half

    def over_z(v, by=1):
        return lax.ppermute(v, "seq", swap(n, lambda z, y, c: (z + by, y, c)))

    def over_y(v):
        return lax.ppermute(v, "seq", swap(n, lambda z, y, c: (z, 1 - y, c)))

    def over_core(v):
        return lax.ppermute(v, "seq", swap(n, lambda z, y, c: (z, y, 1 - c)))

    def over_x(v):
        return lax.ppermute(v, "groups", [(0, 1), (1, 0)])

    p0, rest = kernel(
        dequant_body,
        "scale_rows",
        [struct((shared_rows, columns), BF16), struct((kept, columns), BF16)],
        [HBM, HBM],
        [VMEM, VMEM],
        (frozen, scales.T),
        scratch=[
            pltpu.VMEM((rows, columns), BF16),
            pltpu.SMEM(scales.shape[::-1], F32),
            pltpu.SemaphoreType.DMA((2,)),
        ],
    )
    z1, y0 = over_z(p0), over_y(p0)

    piece = (planes, 2, each, ranks)
    shrink, spread, send, keep = kernel(
        functools.partial(grads_body, rows),
        "gradient_shares",
        [struct((count, ranks), BF16)] * 2 + [struct(piece, F32)] * 2,
        [HBM, VMEM, HBM, HBM, HBM, ANY],
        [VMEM] * 4,
        (tokens, token_adapter_index[None, :], down, up, cotangent, p0),
        scratch=[
            pltpu.VMEM(tokens.shape, BF16),
            pltpu.VMEM(down.shape, BF16),
            pltpu.VMEM(up.shape, BF16),
            pltpu.VMEM(cotangent.shape, BF16),
            pltpu.VMEM((count, ranks), F32),
            pltpu.SemaphoreType.DMA((2 + 2 * planes,)),
        ],
    )

    def plane(k, own, got, state, spread):
        first = k == 0
        kinds = []
        if k == planes - 1:
            kinds = [struct((2, count, kept), BF16), struct((2, kept, ranks), BF16)]
        operands = [tokens, cotangent, spread, down] + own + got
        if first:
            operands += [shrink, up]
            specs = [HBM, VMEM, VMEM, HBM] + [VMEM] * (len(operands) - 4)
            alias = None
        else:
            operands += [state[1], state[0]]
            specs = [HBM, VMEM, VMEM, HBM] + [VMEM] * (len(operands) - 5) + [HBM]
            alias = {len(operands) - 1: 0}
        return kernel(
            functools.partial(plane_body, k, first, rows, kept, (len(own), len(got))),
            f"plane_{k}",
            [struct((count, width), BF16), struct((count, columns), F32)] + kinds,
            specs,
            [HBM, VMEM] + [VMEM] * len(kinds),
            operands,
            scratch=[
                pltpu.VMEM((depth, columns), BF16),
                pltpu.VMEM((count, depth), BF16),
                pltpu.VMEM((count, depth), BF16),
                pltpu.VMEM((depth, ranks), BF16),
                pltpu.SemaphoreType.DMA,
                pltpu.SemaphoreType.DMA((2,)),
            ],
            alias=alias,
        )

    def pack(name, *parts):
        return kernel(
            pack_body,
            name,
            struct((sum(v.shape[0] for v in parts), parts[0].shape[1]), parts[0].dtype),
            [VMEM] * len(parts),
            VMEM,
            parts,
        )

    def last_rows(i, weight, state, saved, spread):
        return kernel(
            functools.partial(last_body, planes - 1, rows, i),
            f"last_rows_{i}",
            [struct((count, width), BF16), struct((count, columns), (F32, BF16)[i])],
            [VMEM] * 6 + [HBM],
            [HBM, VMEM],
            [saved[0], cotangent, spread, saved[1], weight, state[1], state[0]],
            scratch=[pltpu.VMEM((count, kept), BF16), pltpu.SemaphoreType.DMA],
            alias={6: 0},
        )

    def cut(name, v):
        return kernel(
            cut_body, name, struct((kept, columns), BF16), [VMEM], VMEM, (v,)
        )

    core_share = over_core(send)
    z1, spread = hold(z1, spread)
    z2 = over_z(z1)
    y1 = over_y(z1)
    z1, spread = hold(z1, spread)
    cut_z1 = cut("cut_1", z1)
    cut_z1, spread = hold(cut_z1, spread)
    x1a = over_x(cut_z1)
    y0, spread = hold(y0, spread)
    x0 = over_x(y0[:kept])
    core_share, spread = hold(core_share, spread)
    own_y, other_y = kernel(
        core_sum_body,
        "core_sum",
        [struct((planes, each, ranks), F32), struct((planes, each, ranks), BF16)],
        [VMEM] * 2,
        [VMEM] * 2,
        (keep, core_share),
    )
    own_y, spread = hold(own_y, spread)
    side_share = over_y(other_y)
    x1a, spread = hold(x1a, spread)
    y1, spread = hold(y1, spread)
    x1b = over_x(y1[:kept])
    z2, spread = hold(z2, spread)
    z3 = over_z(z2)
    y2 = over_y(z2)
    x2a = over_x(z2[:kept])
    x0, spread = hold(x0, spread)
    side_share, spread = hold(side_share, spread)
    x0, spread = hold(x0, spread)
    pack_0 = pack("pack_0", p0, y0, rest, x0)
    pack_0, spread = hold(pack_0, spread)
    c0 = over_core(pack_0)
    x1b, spread = hold(x1b, spread)
    side_share, spread = hold(side_share, spread)
    line = struct((rows + planes * half, ranks), BF16)
    mine, s1, s2, s3 = kernel(
        functools.partial(side_sum_body, rows),
        "side_sum",
        [struct(line.shape, F32), line, line, line],
        [VMEM] * 2,
        [VMEM] * 4,
        (own_y, side_share),
    )
    mine, spread = hold(mine, spread)
    line_1 = over_z(s1, 1)
    line_2 = over_z(s2, 2)
    line_3 = over_z(s3, 3)
    x1b, spread = hold(x1b, spread)
    pack_1 = pack("pack_1", z1, y1, x1a, x1b)
    pack_1, spread = hold(pack_1, spread)
    c1 = over_core(pack_1)
    z3, spread = hold(z3, spread)
    y3 = over_y(z3)
    x3a = over_x(z3[:kept])
    x2a, spread = hold(x2a, spread)
    c0, spread = hold(c0, spread)
    y2, spread = hold(y2, spread)
    x2b = over_x(y2[:kept])
    line_3, spread = hold(line_3, spread)
    c0, spread = hold(c0, spread)
    act, acc = plane(0, [p0, y0, rest, x0], [c0], None, spread)
    acc, spread = hold(acc, spread)
    c1, spread = hold(c1, spread)
    act, acc = plane(1, [z1, y1, x1a, x1b], [c1], (act, acc), spread)
    acc, spread = hold(acc, spread)
    x3a, spread = hold(x3a, spread)
    y3, spread = hold(y3, spread)
    x3b = over_x(y3[:kept])
    x2b, spread = hold(x2b, spread)
    pack_2 = pack("pack_2", z2, y2, x2a, x2b)
    pack_2, spread = hold(pack_2, spread)
    c2 = over_core(pack_2)
    x3a, spread = hold(x3a, spread)
    pack_3 = pack("pack_3", z3, y3, x3a)
    pack_3, spread = hold(pack_3, spread)
    c3a = over_core(pack_3)
    line_2, spread = hold(line_2, spread)
    line_1, spread = hold(line_1, spread)
    grad_a, quarter = kernel(
        line_sum_body,
        "line_sum",
        [struct((rows, ranks), F32), struct((planes * half, ranks), F32)],
        [VMEM] * 4,
        [VMEM] * 2,
        (mine, line_1, line_2, line_3),
    )
    quarter, spread = hold(quarter, spread)
    side_up = over_y(quarter)
    c2, spread = hold(c2, spread)
    act, acc = plane(2, [z2, y2, x2a, x2b], [c2], (act, acc), spread)
    acc, spread = hold(acc, spread)
    side_up, spread = hold(side_up, spread)
    x3b, spread = hold(x3b, spread)
    c3b = over_core(x3b)
    c3a, spread = hold(c3a, spread)
    side_up, spread = hold(side_up, spread)
    both = pack("pack_up", quarter, side_up)
    both, spread = hold(both, spread)
    core_up = over_core(both)
    c3a, spread = hold(c3a, spread)
    act, acc, *saved = plane(3, [z3, y3, x3a], [c3a], (act, acc), spread)
    acc, spread = hold(acc, spread)
    core_up, spread = hold(core_up, spread)
    grad_b = kernel(
        place_b_body,
        "place_up_gradient",
        struct((ranks, columns), F32),
        [VMEM] * 2,
        VMEM,
        (both, core_up),
    )
    x3b, spread = hold(x3b, spread)
    act, acc = last_rows(0, x3b, (act, acc), saved, spread)
    acc, spread = hold(acc, spread)
    c3b, spread = hold(c3b, spread)
    act, acc = last_rows(1, c3b, (act, acc), saved, spread)
    values = acc
    return values, act, grad_a, grad_b


def solution(mesh):
    sizes = (mesh.shape["groups"], mesh.shape["seq"])

    def on_device(*operands):
        rows, columns = operands[2].shape
        ranks = operands[5].shape[0]
        fits = rows == 5 * STRIP and columns == 8 * ranks
        path = block_path if sizes == (2, 16) and fits and ranks == BLOCK else plain_path
        return path(*operands)

    return jax.shard_map(
        on_device,
        mesh=mesh,
        in_specs=(
            P(("groups", "seq"), None),
            P(("groups", "seq")),
            P("seq", None),
            P(),
            P("groups", None),
            P("groups", None),
            P(("groups", "seq"), None),
        ),
        out_specs=(
            P(("groups", "seq"), None),
            P(("groups", "seq"), None),
            P(("groups", "seq"), None),
            P("groups", None),
        ),
        check_vma=False,
    )
```

```python
import functools

import jax
import jax.numpy as jnp
from jax import lax
from jax.experimental import pallas as pl
from jax.experimental.pallas import tpu as pltpu
from jax.sharding import PartitionSpec as P

BLOCK = 128
ADAPTER_RANK = 16
STRIP = 64
VMEM_LIMIT = 12 * 1024 * 1024
STEP_US = 20
F32 = jnp.float32
BF16 = jnp.bfloat16


def dequant_rows(piece, scales):
    count = piece.shape[0]
    block_of = lax.iota(jnp.int32, count) // BLOCK
    select = (block_of[:, None] == lax.iota(jnp.int32, scales.shape[0])[None, :]).astype(F32)
    row_scales = jnp.dot(select, scales, precision=lax.Precision.HIGHEST)
    expanded = jnp.repeat(row_scales, BLOCK, axis=1)
    return (piece.astype(F32) * expanded).astype(BF16)


def reduce_over_rows(left, right):
    return lax.dot_general(left, right, (((1,), (1,)), ((), ())), preferred_element_type=F32)


def contract_tokens(left, right):
    return lax.dot_general(left, right, (((0,), (0,)), ((), ())), preferred_element_type=F32)


def plain_path(tokens, token_adapter_index, frozen, scales, down, up, cotangent):
    rank_adapter = lax.iota(jnp.int32, down.shape[1]) // ADAPTER_RANK
    mask = (token_adapter_index[:, None] == rank_adapter[None, :]).astype(F32)
    shrink = (jnp.dot(tokens, down, preferred_element_type=F32) * mask).astype(BF16)
    spread = (2.0 * reduce_over_rows(cotangent, up) * mask).astype(BF16)
    weight = dequant_rows(lax.all_gather(frozen, "seq", axis=0, tiled=True), scales)
    values = jnp.dot(tokens, weight, preferred_element_type=F32)
    values = (values + 2.0 * jnp.dot(shrink, up, preferred_element_type=F32)).astype(BF16)
    act = reduce_over_rows(cotangent, weight) + reduce_over_rows(spread, down)
    grad_a = lax.psum_scatter(
        contract_tokens(tokens, spread), "seq", scatter_dimension=0, tiled=True
    )
    grad_b = lax.psum(2.0 * contract_tokens(shrink, cotangent), "seq")
    return values, act.astype(BF16), grad_a, grad_b


OTHER_US = dict(plane_1=0, side_sum=5, pack_0=0, line_sum=0, pack_2=2, pack_up=2, scale_rows=5, gradient_shares=6)
VMEM = pl.BlockSpec(memory_space=pltpu.VMEM)
SMEM = pl.BlockSpec(memory_space=pltpu.SMEM)
ANY = pl.BlockSpec(memory_space=pl.ANY)
HBM = pl.BlockSpec(memory_space=pltpu.HBM)


def struct(shape, dtype):
    return jax.ShapeDtypeStruct(shape, dtype)


def kernel(body, name, out_shape, in_specs, out_specs, operands, scratch=(), alias=None):
    return pl.pallas_call(
        body,
        name=name,
        in_specs=in_specs,
        out_specs=out_specs,
        out_shape=out_shape,
        scratch_shapes=scratch,
        input_output_aliases=alias or {},
        compiler_params=pltpu.CompilerParams(vmem_limit_bytes=VMEM_LIMIT),
        cost_estimate=pl.CostEstimate(
            flops=int(OTHER_US.get(name, STEP_US) * 1.1e9), bytes_accessed=1, transcendentals=0
        ),
    )(*operands)


def hold(value, after):
    return lax.optimization_barrier((value, after))


def place():
    s = lax.axis_index("seq")
    return s // 4, s // 2 % 2, s % 2, lax.axis_index("groups")


def strip_places(core, x):
    low = core * STRIP
    return low + x * (2 * STRIP), (1 - core) * (4 * STRIP), low + (1 - x) * (2 * STRIP)


def fetch(pairs, sems):
    copies = [pltpu.make_async_copy(a, b, sems.at[i]) for i, (a, b) in enumerate(pairs)]
    for copy in copies:
        copy.start()
    return copies


def dequant_body(w_far, scales_far, shared, rest, w, scales, sems):
    for copy in fetch(((scales_far, scales), (w_far, w)), sems):
        copy.wait()
    z, y, c, x = place()
    first = ((z * 2 + y) * 2 + c) * (w.shape[0] // STRIP)

    def scale_strips(out, at, count, source):
        for i in range(count // STRIP):
            start = source + i * STRIP
            block_row = (first * STRIP + start) // BLOCK
            rows = pl.ds(pl.multiple_of(start, STRIP), STRIP)
            for b in range(w.shape[1] // BLOCK):
                columns = pl.ds(b * BLOCK, BLOCK)
                value = w[rows, columns].astype(F32) * scales[b, block_row]
                out[pl.ds(at + i * STRIP, STRIP), columns] = value.astype(BF16)

    kept = rest.shape[0]
    mine, middle, other = strip_places(c, x)
    scale_strips(shared, 0, kept, mine)
    scale_strips(shared, kept, shared.shape[0] - kept, middle)
    scale_strips(rest, 0, kept, other)


def grads_body(rows, tok_far, idx, down_far, up_far, cot_far, _, *refs):
    shrink, spread, send, keep, tok, down, up, cot, acc, sems = refs
    c = place()[2]
    ranks, planes = up.shape[0], send.shape[0]
    depth = tok.shape[1] // planes
    half = ranks // 2
    pairs = [(up_far, up), (cot_far, cot)]
    for j in range(planes):
        part = pl.ds(j * depth, depth)
        pairs += [(tok_far.at[:, part], tok.at[:, part]), (down_far.at[part, :], down.at[part, :])]
    copies = fetch(pairs, sems)
    rank_adapter = lax.broadcasted_iota(jnp.int32, (ranks, 1), 0) // ADAPTER_RANK
    mask = (idx[...] == rank_adapter).astype(F32).T
    copies[0].wait()
    copies[1].wait()
    spread[...] = (2.0 * reduce_over_rows(cot[...], up[...]) * mask).astype(BF16)

    def store(j, y, core, at, value):
        @pl.when(c == core)
        def _():
            keep[j, y, pl.ds(at, value.shape[0]), :] = value

        @pl.when(c != core)
        def _():
            send[j, y, pl.ds(at, value.shape[0]), :] = value

    for j in range(planes):
        copies[2 + 2 * j].wait()
        copies[3 + 2 * j].wait()
        block = tok[:, j * depth : (j + 1) * depth]
        sum_j = jnp.dot(block, down[j * depth : (j + 1) * depth], preferred_element_type=F32)
        if j == 0:
            acc[...] = sum_j
        else:
            acc[...] += sum_j
        part = contract_tokens(block, spread[...])
        for y in range(2):
            for core in range(2):
                at = (y * 2 + core) * rows
                store(j, y, core, 0, part[at : at + rows])
    shrink[...] = (acc[...] * mask).astype(BF16)
    grad_b = contract_tokens(shrink[...], cot[...])
    for y in range(2):
        for j in range(planes):
            at = (y * planes + j) * ranks
            for core in range(2):
                piece = grad_b[core * half : (core + 1) * half, at : at + ranks]
                store(j, y, core, rows, piece)


def core_sum_body(keep, got, own, other):
    y = place()[1]
    for j in range(keep.shape[0]):
        own[j] = keep[j, y] + got[j, y]
        other[j] = (keep[j, 1 - y] + got[j, 1 - y]).astype(BF16)


def side_sum_body(rows, own, got, mine, s1, s2, s3):
    z = place()[0]
    planes, each = own.shape[:2]
    half = each - rows
    a_part = pl.ds(0, rows)
    for step, out in enumerate((mine, s1, s2, s3)):
        to = lax.rem(z + step, planes)
        piece = own[to, a_part, :] + got[to, a_part, :].astype(F32)
        out[pl.ds(0, rows), :] = piece.astype(out.dtype)
    for j in range(planes):
        piece = own[j, pl.ds(rows, half), :] + got[j, pl.ds(rows, half), :].astype(F32)
        piece = piece.astype(BF16)
        for out in (mine, s1, s2, s3):
            out[pl.ds(rows + j * half, half), :] = piece.astype(out.dtype)


def line_sum_body(mine, r1, r2, r3, grad_a, quarter):
    rows = grad_a.shape[0]
    total = (mine[...] + r2[...].astype(F32)) + (r1[...].astype(F32) + r3[...].astype(F32))
    grad_a[...] = total[:rows]
    quarter[...] = 2.0 * total[rows:]


def place_b(mine, core, out):
    _, y, c, _ = place()
    ranks = out.shape[0]
    half = ranks // 2
    planes = mine.shape[0] // (2 * half)
    for ref, cc in ((mine, c), (core, 1 - c)):
        row = pl.multiple_of(cc * half, half)
        for j in range(2 * planes):
            yy = y if j < planes else 1 - y
            column = pl.multiple_of((yy * planes + j % planes) * ranks, ranks)
            out[pl.ds(row, half), pl.ds(column, ranks)] = ref[pl.ds(j * half, half), :]


def plane_body(k, first, rows, kept, counts, tok_far, cot, spread, down_far, *refs):
    pieces, refs = refs[: sum(counts)], refs[sum(counts) :]
    if first:
        shrink, up, act, acc, *saved, weight, block, tok, down, sem, sems = refs
    else:
        total, _, act, acc, *saved, weight, block, tok, down, sem, sems = refs
    z, y, c, x = place()
    depth = weight.shape[0]
    zz = lax.rem(z + 4 - k, 4)
    columns = pl.ds(pl.multiple_of(zz * depth, depth), depth)
    copies = fetch(((down_far.at[columns, :], down), (tok_far.at[:, columns], tok)), sems)
    middle = rows - 2 * kept

    def put(ref, at, count, to):
        weight[pl.ds(pl.multiple_of(to, STRIP), count), :] = ref[pl.ds(at, count), :]

    for h, cc in enumerate((c, 1 - c)):
        own = pieces[: counts[0]] if h == 0 else pieces[counts[0] :]
        where = []
        for ref in own:
            where += [(ref, at) for at in range(0, ref.shape[0], STRIP)]
        strips = iter(where)
        bases = [((y if i == 0 else 1 - y) * 2 + cc) * rows for i in range(2)]
        mine, inner, other = strip_places(cc, x)

        def next_strips(count, to):
            for i in range(count // STRIP):
                ref, at = next(strips, (None, 0))
                if ref is None:
                    here = pl.ds(pl.multiple_of(to + i * STRIP, STRIP), STRIP)
                    weight[here, :] = jnp.zeros((STRIP, weight.shape[1]), BF16)
                else:
                    put(ref, at, STRIP, to + i * STRIP)

        for base in bases:
            next_strips(kept, base + mine)
            next_strips(middle, base + inner)
        for base in bases:
            next_strips(kept, base + other)

    back = reduce_over_rows(cot[...], weight[...])
    copies[0].wait()
    back += reduce_over_rows(spread[...], down[...])
    block[...] = back.astype(BF16)
    copy = pltpu.make_async_copy(block, act.at[:, columns], sem)
    copy.start()
    copies[1].wait()
    forward = jnp.dot(tok[...], weight[...], preferred_element_type=F32)
    if first:
        forward += 2.0 * jnp.dot(shrink[...], up[...], preferred_element_type=F32)
    else:
        forward += total[...]
    acc[...] = forward
    if saved:
        for i in range(2):
            here = pl.ds(late_rows(k, rows, i, x, z, y, c)[0], kept)
            saved[0][i] = tok[:, here]
            saved[1][i] = down[here, :]
    copy.wait()


def late_rows(k, rows, i, x, z, y, c):
    cc = c if i == 0 else 1 - c
    within = ((1 - y) * 2 + cc) * rows + strip_places(cc, x)[2]
    zz = lax.rem(z + 4 - k, 4)
    return pl.multiple_of(within, BLOCK), pl.multiple_of(zz * 4 * rows + within, BLOCK)


def last_body(k, rows, i, tok, cot, spread, down, weight, total, *refs):
    if i == 0:
        _, act, out, block, sems = refs
    else:
        both, core_up, _, act, out, grad_b, block, values, placed, sems = refs
    z, y, c, x = place()
    kept = weight.shape[0]
    start = late_rows(k, rows, i, x, z, y, c)[1]
    copies = []

    def send(source, target):
        copies.append(pltpu.make_async_copy(source, target, sems.at[len(copies)]))
        copies[-1].start()

    if i == 1:
        place_b(both, core_up, placed)
        send(placed, grad_b)
    back = reduce_over_rows(cot[...], weight[...])
    back += reduce_over_rows(spread[...], down[i])
    block[...] = back.astype(BF16)
    send(block, act.at[:, pl.ds(start, kept)])
    if i == 0:
        out[...] = total[...] + jnp.dot(tok[i], weight[...], preferred_element_type=F32)
    else:
        step = weight.shape[1] // 2
        for at in range(0, weight.shape[1], step):
            here = pl.ds(at, step)
            forward = jnp.dot(tok[i], weight[:, here], preferred_element_type=F32)
            values[:, here] = (total[:, here] + forward).astype(BF16)
            send(values.at[:, here], out.at[:, here])
    for copy in copies:
        copy.wait()


def cut_body(ref, out):
    out[...] = ref[pl.ds(0, out.shape[0]), :]


def pack_body(*refs):
    out, at = refs[-1], 0
    for ref in refs[:-1]:
        out[pl.ds(at, ref.shape[0]), :] = ref[...]
        at += ref.shape[0]


def swap(n, move):
    pairs = []
    for s in range(n):
        z, y, c = move(s // 4, s // 2 % 2, s % 2)
        pairs.append((s, (z % (n // 4) * 2 + y) * 2 + c))
    return pairs


def block_path(tokens, token_adapter_index, frozen, scales, down, up, cotangent):
    n, planes = 16, 4
    count, width = tokens.shape
    rows, columns = frozen.shape
    ranks = up.shape[0]
    depth = width // planes
    kept = 2 * STRIP
    shared_rows = rows - kept
    half = ranks // 2
    each = rows + half

    def over_z(v, by=1):
        return lax.ppermute(v, "seq", swap(n, lambda z, y, c: (z + by, y, c)))

    def over_y(v):
        return lax.ppermute(v, "seq", swap(n, lambda z, y, c: (z, 1 - y, c)))

    def over_core(v):
        return lax.ppermute(v, "seq", swap(n, lambda z, y, c: (z, y, 1 - c)))

    def over_x(v):
        return lax.ppermute(v, "groups", [(0, 1), (1, 0)])

    p0, rest = kernel(
        dequant_body,
        "scale_rows",
        [struct((shared_rows, columns), BF16), struct((kept, columns), BF16)],
        [HBM, HBM],
        [VMEM, VMEM],
        (frozen, scales.T),
        scratch=[
            pltpu.VMEM((rows, columns), BF16),
            pltpu.SMEM(scales.shape[::-1], F32),
            pltpu.SemaphoreType.DMA((2,)),
        ],
    )
    z1, y0 = over_z(p0), over_y(p0)

    piece = (planes, 2, each, ranks)
    shrink, spread, send, keep = kernel(
        functools.partial(grads_body, rows),
        "gradient_shares",
        [struct((count, ranks), BF16)] * 2 + [struct(piece, F32)] * 2,
        [HBM, VMEM, HBM, HBM, HBM, ANY],
        [VMEM] * 4,
        (tokens, token_adapter_index[None, :], down, up, cotangent, p0),
        scratch=[
            pltpu.VMEM(tokens.shape, BF16),
            pltpu.VMEM(down.shape, BF16),
            pltpu.VMEM(up.shape, BF16),
            pltpu.VMEM(cotangent.shape, BF16),
            pltpu.VMEM((count, ranks), F32),
            pltpu.SemaphoreType.DMA((2 + 2 * planes,)),
        ],
    )

    def plane(k, own, got, state, spread):
        first = k == 0
        kinds = []
        if k == planes - 1:
            kinds = [struct((2, count, kept), BF16), struct((2, kept, ranks), BF16)]
        operands = [tokens, cotangent, spread, down] + own + got
        if first:
            operands += [shrink, up]
            specs = [HBM, VMEM, VMEM, HBM] + [VMEM] * (len(operands) - 4)
            alias = None
        else:
            operands += [state[1], state[0]]
            specs = [HBM, VMEM, VMEM, HBM] + [VMEM] * (len(operands) - 5) + [HBM]
            alias = {len(operands) - 1: 0}
        return kernel(
            functools.partial(plane_body, k, first, rows, kept, (len(own), len(got))),
            f"plane_{k}",
            [struct((count, width), BF16), struct((count, columns), F32)] + kinds,
            specs,
            [HBM, VMEM] + [VMEM] * len(kinds),
            operands,
            scratch=[
                pltpu.VMEM((depth, columns), BF16),
                pltpu.VMEM((count, depth), BF16),
                pltpu.VMEM((count, depth), BF16),
                pltpu.VMEM((depth, ranks), BF16),
                pltpu.SemaphoreType.DMA,
                pltpu.SemaphoreType.DMA((2,)),
            ],
            alias=alias,
        )

    def pack(name, *parts):
        return kernel(
            pack_body,
            name,
            struct((sum(v.shape[0] for v in parts), parts[0].shape[1]), parts[0].dtype),
            [VMEM] * len(parts),
            VMEM,
            parts,
        )

    def last_rows(i, weight, state, saved, spread, *gradient):
        kinds = [struct((count, width), BF16)]
        scratch = [pltpu.VMEM((count, kept), BF16)]
        if i == 0:
            kinds += [struct((count, columns), F32)]
        else:
            kinds += [struct((count, columns), BF16), struct((ranks, columns), F32)]
            scratch += [pltpu.VMEM((count, columns), BF16), pltpu.VMEM((ranks, columns), F32)]
        operands = [saved[0], cotangent, spread, saved[1], weight, state[1], *gradient, state[0]]
        return kernel(
            functools.partial(last_body, planes - 1, rows, i),
            f"last_rows_{i}",
            kinds,
            [VMEM] * (len(operands) - 1) + [HBM],
            [HBM, VMEM] if i == 0 else [HBM] * 3,
            operands,
            scratch=scratch + [pltpu.SemaphoreType.DMA((1 if i == 0 else 4,))],
            alias={len(operands) - 1: 0},
        )

    def cut(name, v):
        return kernel(
            cut_body, name, struct((kept, columns), BF16), [VMEM], VMEM, (v,)
        )

    core_share = over_core(send)
    z1, spread = hold(z1, spread)
    z2 = over_z(z1)
    y1 = over_y(z1)
    z1, spread = hold(z1, spread)
    cut_z1 = cut("cut_1", z1)
    cut_z1, spread = hold(cut_z1, spread)
    x1a = over_x(cut_z1)
    y0, spread = hold(y0, spread)
    x0 = over_x(y0[:kept])
    core_share, spread = hold(core_share, spread)
    own_y, other_y = kernel(
        core_sum_body,
        "core_sum",
        [struct((planes, each, ranks), F32), struct((planes, each, ranks), BF16)],
        [VMEM] * 2,
        [VMEM] * 2,
        (keep, core_share),
    )
    own_y, spread = hold(own_y, spread)
    side_share = over_y(other_y)
    x1a, spread = hold(x1a, spread)
    y1, spread = hold(y1, spread)
    x1b = over_x(y1[:kept])
    z2, spread = hold(z2, spread)
    z3 = over_z(z2)
    y2 = over_y(z2)
    x2a = over_x(z2[:kept])
    x0, spread = hold(x0, spread)
    side_share, spread = hold(side_share, spread)
    x0, spread = hold(x0, spread)
    pack_0 = pack("pack_0", p0, y0, rest, x0)
    pack_0, spread = hold(pack_0, spread)
    c0 = over_core(pack_0)
    x1b, spread = hold(x1b, spread)
    side_share, spread = hold(side_share, spread)
    line = struct((rows + planes * half, ranks), BF16)
    mine, s1, s2, s3 = kernel(
        functools.partial(side_sum_body, rows),
        "side_sum",
        [struct(line.shape, F32), line, line, line],
        [VMEM] * 2,
        [VMEM] * 4,
        (own_y, side_share),
    )
    mine, spread = hold(mine, spread)
    line_1 = over_z(s1, 1)
    line_2 = over_z(s2, 2)
    line_3 = over_z(s3, 3)
    x1b, spread = hold(x1b, spread)
    pack_1 = pack("pack_1", z1, y1, x1a, x1b)
    pack_1, spread = hold(pack_1, spread)
    c1 = over_core(pack_1)
    z3, spread = hold(z3, spread)
    y3 = over_y(z3)
    x3a = over_x(z3[:kept])
    x2a, spread = hold(x2a, spread)
    c0, spread = hold(c0, spread)
    y2, spread = hold(y2, spread)
    x2b = over_x(y2[:kept])
    line_3, spread = hold(line_3, spread)
    c0, spread = hold(c0, spread)
    act, acc = plane(0, [p0, y0, rest, x0], [c0], None, spread)
    acc, spread = hold(acc, spread)
    c1, spread = hold(c1, spread)
    act, acc = plane(1, [z1, y1, x1a, x1b], [c1], (act, acc), spread)
    acc, spread = hold(acc, spread)
    x3a, spread = hold(x3a, spread)
    y3, spread = hold(y3, spread)
    x3b = over_x(y3[:kept])
    x2b, spread = hold(x2b, spread)
    pack_2 = pack("pack_2", z2, y2, x2a, x2b)
    pack_2, spread = hold(pack_2, spread)
    c2 = over_core(pack_2)
    x3a, spread = hold(x3a, spread)
    pack_3 = pack("pack_3", z3, y3, x3a)
    pack_3, spread = hold(pack_3, spread)
    c3a = over_core(pack_3)
    line_2, spread = hold(line_2, spread)
    line_1, spread = hold(line_1, spread)
    grad_a, quarter = kernel(
        line_sum_body,
        "line_sum",
        [struct((rows, ranks), F32), struct((planes * half, ranks), F32)],
        [VMEM] * 4,
        [VMEM] * 2,
        (mine, line_1, line_2, line_3),
    )
    quarter, spread = hold(quarter, spread)
    side_up = over_y(quarter)
    c2, spread = hold(c2, spread)
    act, acc = plane(2, [z2, y2, x2a, x2b], [c2], (act, acc), spread)
    acc, spread = hold(acc, spread)
    c3a, spread = hold(c3a, spread)
    act, acc, *saved = plane(3, [z3, y3, x3a], [c3a], (act, acc), spread)
    acc, spread = hold(acc, spread)
    side_up, spread = hold(side_up, spread)
    both = pack("pack_up", quarter, side_up)
    both, spread = hold(both, spread)
    core_up = over_core(both)
    x3b, spread = hold(x3b, spread)
    c3b = over_core(x3b)
    act, acc = last_rows(0, x3b, (act, acc), saved, spread)
    acc, spread = hold(acc, spread)
    core_up, spread = hold(core_up, spread)
    c3b, spread = hold(c3b, spread)
    act, values, grad_b = last_rows(1, c3b, (act, acc), saved, spread, both, core_up)
    return values, act, grad_a, grad_b


def solution(mesh):
    sizes = (mesh.shape["groups"], mesh.shape["seq"])

    def on_device(*operands):
        rows, columns = operands[2].shape
        ranks = operands[5].shape[0]
        fits = rows == 5 * STRIP and columns == 8 * ranks
        path = block_path if sizes == (2, 16) and fits and ranks == BLOCK else plain_path
        return path(*operands)

    return jax.shard_map(
        on_device,
        mesh=mesh,
        in_specs=(
            P(("groups", "seq"), None),
            P(("groups", "seq")),
            P("seq", None),
            P(),
            P("groups", None),
            P("groups", None),
            P(("groups", "seq"), None),
        ),
        out_specs=(
            P(("groups", "seq"), None),
            P(("groups", "seq"), None),
            P(("groups", "seq"), None),
            P("groups", None),
        ),
        check_vma=False,
    )
```

```python
import functools

import jax
import jax.numpy as jnp
from jax import lax
from jax.experimental import pallas as pl
from jax.experimental.pallas import tpu as pltpu
from jax.sharding import PartitionSpec as P

BLOCK = 128
ADAPTER_RANK = 16
STRIP = 64
VMEM_LIMIT = 12 * 1024 * 1024
STEP_US = 20
F32 = jnp.float32
BF16 = jnp.bfloat16


def dequant_rows(piece, scales):
    count = piece.shape[0]
    block_of = lax.iota(jnp.int32, count) // BLOCK
    select = (block_of[:, None] == lax.iota(jnp.int32, scales.shape[0])[None, :]).astype(F32)
    row_scales = jnp.dot(select, scales, precision=lax.Precision.HIGHEST)
    expanded = jnp.repeat(row_scales, BLOCK, axis=1)
    return (piece.astype(F32) * expanded).astype(BF16)


def reduce_over_rows(left, right):
    return lax.dot_general(left, right, (((1,), (1,)), ((), ())), preferred_element_type=F32)


def contract_tokens(left, right):
    return lax.dot_general(left, right, (((0,), (0,)), ((), ())), preferred_element_type=F32)


def plain_path(tokens, token_adapter_index, frozen, scales, down, up, cotangent):
    rank_adapter = lax.iota(jnp.int32, down.shape[1]) // ADAPTER_RANK
    mask = (token_adapter_index[:, None] == rank_adapter[None, :]).astype(F32)
    shrink = (jnp.dot(tokens, down, preferred_element_type=F32) * mask).astype(BF16)
    spread = (2.0 * reduce_over_rows(cotangent, up) * mask).astype(BF16)
    weight = dequant_rows(lax.all_gather(frozen, "seq", axis=0, tiled=True), scales)
    values = jnp.dot(tokens, weight, preferred_element_type=F32)
    values = (values + 2.0 * jnp.dot(shrink, up, preferred_element_type=F32)).astype(BF16)
    act = reduce_over_rows(cotangent, weight) + reduce_over_rows(spread, down)
    grad_a = lax.psum_scatter(
        contract_tokens(tokens, spread), "seq", scatter_dimension=0, tiled=True
    )
    grad_b = lax.psum(2.0 * contract_tokens(shrink, cotangent), "seq")
    return values, act.astype(BF16), grad_a, grad_b


OTHER_US = dict(plane_1=0, side_sum=5, pack_0=0, line_sum=0, pack_2=2, pack_up=2, scale_rows=5, gradient_shares=6)
VMEM = pl.BlockSpec(memory_space=pltpu.VMEM)
SMEM = pl.BlockSpec(memory_space=pltpu.SMEM)
ANY = pl.BlockSpec(memory_space=pl.ANY)
HBM = pl.BlockSpec(memory_space=pltpu.HBM)


def struct(shape, dtype):
    return jax.ShapeDtypeStruct(shape, dtype)


def kernel(body, name, out_shape, in_specs, out_specs, operands, scratch=(), alias=None):
    return pl.pallas_call(
        body,
        name=name,
        in_specs=in_specs,
        out_specs=out_specs,
        out_shape=out_shape,
        scratch_shapes=scratch,
        input_output_aliases=alias or {},
        compiler_params=pltpu.CompilerParams(vmem_limit_bytes=VMEM_LIMIT),
        cost_estimate=pl.CostEstimate(
            flops=int(OTHER_US.get(name, STEP_US) * 1.1e9), bytes_accessed=1, transcendentals=0
        ),
    )(*operands)


def hold(value, after):
    return lax.optimization_barrier((value, after))


def place():
    s = lax.axis_index("seq")
    return s // 4, s // 2 % 2, s % 2, lax.axis_index("groups")


def strip_places(core, x):
    low = core * STRIP
    return low + x * (2 * STRIP), (1 - core) * (4 * STRIP), low + (1 - x) * (2 * STRIP)


def fetch(pairs, sems):
    copies = [pltpu.make_async_copy(a, b, sems.at[i]) for i, (a, b) in enumerate(pairs)]
    for copy in copies:
        copy.start()
    return copies


def dequant_body(w_far, scales_far, shared, rest, w, scales, sems):
    for copy in fetch(((scales_far, scales), (w_far, w)), sems):
        copy.wait()
    z, y, c, x = place()
    first = ((z * 2 + y) * 2 + c) * (w.shape[0] // STRIP)

    def scale_strips(out, at, count, source):
        for i in range(count // STRIP):
            start = source + i * STRIP
            block_row = (first * STRIP + start) // BLOCK
            rows = pl.ds(pl.multiple_of(start, STRIP), STRIP)
            for b in range(w.shape[1] // BLOCK):
                columns = pl.ds(b * BLOCK, BLOCK)
                value = w[rows, columns].astype(F32) * scales[b, block_row]
                out[pl.ds(at + i * STRIP, STRIP), columns] = value.astype(BF16)

    kept = rest.shape[0]
    mine, middle, other = strip_places(c, x)
    scale_strips(shared, 0, kept, mine)
    scale_strips(shared, kept, shared.shape[0] - kept, middle)
    scale_strips(rest, 0, kept, other)


def grads_body(rows, tok_far, idx, down_far, up_far, cot_far, _, *refs):
    shrink, spread, send, keep, tok, down, up, cot, acc, sems = refs
    c = place()[2]
    ranks, planes = up.shape[0], send.shape[0]
    depth = tok.shape[1] // planes
    half = ranks // 2
    pairs = [(up_far, up), (cot_far, cot)]
    for j in range(planes):
        part = pl.ds(j * depth, depth)
        pairs += [(tok_far.at[:, part], tok.at[:, part]), (down_far.at[part, :], down.at[part, :])]
    copies = fetch(pairs, sems)
    rank_adapter = lax.broadcasted_iota(jnp.int32, (ranks, 1), 0) // ADAPTER_RANK
    mask = (idx[...] == rank_adapter).astype(F32).T
    copies[0].wait()
    copies[1].wait()
    spread[...] = (2.0 * reduce_over_rows(cot[...], up[...]) * mask).astype(BF16)

    def store(j, y, core, at, value):
        @pl.when(c == core)
        def _():
            keep[j, y, pl.ds(at, value.shape[0]), :] = value

        @pl.when(c != core)
        def _():
            send[j, y, pl.ds(at, value.shape[0]), :] = value

    for j in range(planes):
        copies[2 + 2 * j].wait()
        copies[3 + 2 * j].wait()
        block = tok[:, j * depth : (j + 1) * depth]
        sum_j = jnp.dot(block, down[j * depth : (j + 1) * depth], preferred_element_type=F32)
        if j == 0:
            acc[...] = sum_j
        else:
            acc[...] += sum_j
        part = contract_tokens(block, spread[...])
        for y in range(2):
            for core in range(2):
                at = (y * 2 + core) * rows
                store(j, y, core, 0, part[at : at + rows])
    shrink[...] = (acc[...] * mask).astype(BF16)
    grad_b = contract_tokens(shrink[...], cot[...])
    for y in range(2):
        for j in range(planes):
            at = (y * planes + j) * ranks
            for core in range(2):
                piece = grad_b[core * half : (core + 1) * half, at : at + ranks]
                store(j, y, core, rows, piece)


def core_sum_body(keep, got, own, other):
    y = place()[1]
    for j in range(keep.shape[0]):
        own[j] = keep[j, y] + got[j, y]
        other[j] = (keep[j, 1 - y] + got[j, 1 - y]).astype(BF16)


def side_sum_body(rows, own, got, mine, s1, s2, s3):
    z = place()[0]
    planes, each = own.shape[:2]
    half = each - rows
    a_part = pl.ds(0, rows)
    for step, out in enumerate((mine, s1, s2, s3)):
        to = lax.rem(z + step, planes)
        piece = own[to, a_part, :] + got[to, a_part, :].astype(F32)
        out[pl.ds(0, rows), :] = piece.astype(out.dtype)
    for j in range(planes):
        piece = own[j, pl.ds(rows, half), :] + got[j, pl.ds(rows, half), :].astype(F32)
        piece = piece.astype(BF16)
        for out in (mine, s1, s2, s3):
            out[pl.ds(rows + j * half, half), :] = piece.astype(out.dtype)


def line_sum_body(mine, r1, r2, r3, grad_a, quarter):
    rows = grad_a.shape[0]
    total = (mine[...] + r2[...].astype(F32)) + (r1[...].astype(F32) + r3[...].astype(F32))
    grad_a[...] = total[:rows]
    quarter[...] = 2.0 * total[rows:]


def place_b(mine, core, out):
    _, y, c, _ = place()
    ranks = out.shape[0]
    half = ranks // 2
    planes = mine.shape[0] // (2 * half)
    for ref, cc in ((mine, c), (core, 1 - c)):
        row = pl.multiple_of(cc * half, half)
        for j in range(2 * planes):
            yy = y if j < planes else 1 - y
            column = pl.multiple_of((yy * planes + j % planes) * ranks, ranks)
            out[pl.ds(row, half), pl.ds(column, ranks)] = ref[pl.ds(j * half, half), :]


def plane_body(k, first, rows, kept, counts, tok_far, cot, spread, down_far, *refs):
    pieces, refs = refs[: sum(counts)], refs[sum(counts) :]
    if first:
        shrink, up, act, acc, *saved, weight, block, tok, down, sem, sems = refs
    else:
        total, _, act, acc, *saved, weight, block, tok, down, sem, sems = refs
    z, y, c, x = place()
    depth = weight.shape[0]
    zz = lax.rem(z + 4 - k, 4)
    columns = pl.ds(pl.multiple_of(zz * depth, depth), depth)
    copies = fetch(((down_far.at[columns, :], down), (tok_far.at[:, columns], tok)), sems)
    middle = rows - 2 * kept

    def put(ref, at, count, to):
        weight[pl.ds(pl.multiple_of(to, STRIP), count), :] = ref[pl.ds(at, count), :]

    for h, cc in enumerate((c, 1 - c)):
        own = pieces[: counts[0]] if h == 0 else pieces[counts[0] :]
        where = []
        for ref in own:
            where += [(ref, at) for at in range(0, ref.shape[0], STRIP)]
        strips = iter(where)
        bases = [((y if i == 0 else 1 - y) * 2 + cc) * rows for i in range(2)]
        mine, inner, other = strip_places(cc, x)

        def next_strips(count, to):
            for i in range(count // STRIP):
                ref, at = next(strips, (None, 0))
                if ref is None:
                    here = pl.ds(pl.multiple_of(to + i * STRIP, STRIP), STRIP)
                    weight[here, :] = jnp.zeros((STRIP, weight.shape[1]), BF16)
                else:
                    put(ref, at, STRIP, to + i * STRIP)

        for base in bases:
            next_strips(kept, base + mine)
            next_strips(middle, base + inner)
        for base in bases:
            next_strips(kept, base + other)

    back = reduce_over_rows(cot[...], weight[...])
    copies[0].wait()
    back += reduce_over_rows(spread[...], down[...])
    block[...] = back.astype(BF16)
    copy = pltpu.make_async_copy(block, act.at[:, columns], sem)
    copy.start()
    copies[1].wait()
    forward = jnp.dot(tok[...], weight[...], preferred_element_type=F32)
    if first:
        forward += 2.0 * jnp.dot(shrink[...], up[...], preferred_element_type=F32)
    else:
        forward += total[...]
    acc[...] = forward
    if saved:
        for i in range(2):
            here = pl.ds(late_rows(k, rows, i, x, z, y, c)[0], kept)
            saved[0][i] = tok[:, here]
            saved[1][i] = down[here, :]
    copy.wait()


def late_rows(k, rows, i, x, z, y, c):
    cc = c if i == 0 else 1 - c
    within = ((1 - y) * 2 + cc) * rows + strip_places(cc, x)[2]
    zz = lax.rem(z + 4 - k, 4)
    return pl.multiple_of(within, BLOCK), pl.multiple_of(zz * 4 * rows + within, BLOCK)


def last_body(k, rows, i, tok, cot, spread, down, weight, total, *refs):
    if i == 0:
        _, act, out, block, sems = refs
    else:
        both, core_up, _, act, out, grad_b, block, values, placed, sems = refs
    z, y, c, x = place()
    kept = weight.shape[0]
    start = late_rows(k, rows, i, x, z, y, c)[1]
    copies = []

    def send(source, target):
        copies.append(pltpu.make_async_copy(source, target, sems.at[len(copies)]))
        copies[-1].start()

    if i == 1:
        place_b(both, core_up, placed)
        send(placed, grad_b)
    back = reduce_over_rows(cot[...], weight[...])
    back += reduce_over_rows(spread[...], down[i])
    block[...] = back.astype(BF16)
    send(block, act.at[:, pl.ds(start, kept)])
    if i == 0:
        out[...] = total[...] + jnp.dot(tok[i], weight[...], preferred_element_type=F32)
    else:
        step = weight.shape[1] // 2
        for at in range(0, weight.shape[1], step):
            here = pl.ds(at, step)
            forward = jnp.dot(tok[i], weight[:, here], preferred_element_type=F32)
            values[:, here] = (total[:, here] + forward).astype(BF16)
            send(values.at[:, here], out.at[:, here])
    for copy in copies:
        copy.wait()


def cut_body(ref, out):
    out[...] = ref[pl.ds(0, out.shape[0]), :]


def pack_body(*refs):
    out, at = refs[-1], 0
    for ref in refs[:-1]:
        out[pl.ds(at, ref.shape[0]), :] = ref[...]
        at += ref.shape[0]


def swap(n, move):
    pairs = []
    for s in range(n):
        z, y, c = move(s // 4, s // 2 % 2, s % 2)
        pairs.append((s, (z % (n // 4) * 2 + y) * 2 + c))
    return pairs


def block_path(tokens, token_adapter_index, frozen, scales, down, up, cotangent):
    n, planes = 16, 4
    count, width = tokens.shape
    rows, columns = frozen.shape
    ranks = up.shape[0]
    depth = width // planes
    kept = 2 * STRIP
    shared_rows = rows - kept
    half = ranks // 2
    each = rows + half

    def over_z(v, by=1):
        return lax.ppermute(v, "seq", swap(n, lambda z, y, c: (z + by, y, c)))

    def over_y(v):
        return lax.ppermute(v, "seq", swap(n, lambda z, y, c: (z, 1 - y, c)))

    def over_core(v):
        return lax.ppermute(v, "seq", swap(n, lambda z, y, c: (z, y, 1 - c)))

    def over_x(v):
        return lax.ppermute(v, "groups", [(0, 1), (1, 0)])

    p0, rest = kernel(
        dequant_body,
        "scale_rows",
        [struct((shared_rows, columns), BF16), struct((kept, columns), BF16)],
        [HBM, HBM],
        [VMEM, VMEM],
        (frozen, scales.T),
        scratch=[
            pltpu.VMEM((rows, columns), BF16),
            pltpu.SMEM(scales.shape[::-1], F32),
            pltpu.SemaphoreType.DMA((2,)),
        ],
    )
    z1, y0 = over_z(p0), over_y(p0)

    piece = (planes, 2, each, ranks)
    shrink, spread, send, keep = kernel(
        functools.partial(grads_body, rows),
        "gradient_shares",
        [struct((count, ranks), BF16)] * 2 + [struct(piece, F32)] * 2,
        [HBM, VMEM, HBM, HBM, HBM, ANY],
        [VMEM] * 4,
        (tokens, token_adapter_index[None, :], down, up, cotangent, p0),
        scratch=[
            pltpu.VMEM(tokens.shape, BF16),
            pltpu.VMEM(down.shape, BF16),
            pltpu.VMEM(up.shape, BF16),
            pltpu.VMEM(cotangent.shape, BF16),
            pltpu.VMEM((count, ranks), F32),
            pltpu.SemaphoreType.DMA((2 + 2 * planes,)),
        ],
    )

    def plane(k, own, got, state, spread):
        first = k == 0
        kinds = []
        if k == planes - 1:
            kinds = [struct((2, count, kept), BF16), struct((2, kept, ranks), BF16)]
        operands = [tokens, cotangent, spread, down] + own + got
        if first:
            operands += [shrink, up]
            specs = [HBM, VMEM, VMEM, HBM] + [VMEM] * (len(operands) - 4)
            alias = None
        else:
            operands += [state[1], state[0]]
            specs = [HBM, VMEM, VMEM, HBM] + [VMEM] * (len(operands) - 5) + [HBM]
            alias = {len(operands) - 1: 0}
        return kernel(
            functools.partial(plane_body, k, first, rows, kept, (len(own), len(got))),
            f"plane_{k}",
            [struct((count, width), BF16), struct((count, columns), F32)] + kinds,
            specs,
            [HBM, VMEM] + [VMEM] * len(kinds),
            operands,
            scratch=[
                pltpu.VMEM((depth, columns), BF16),
                pltpu.VMEM((count, depth), BF16),
                pltpu.VMEM((count, depth), BF16),
                pltpu.VMEM((depth, ranks), BF16),
                pltpu.SemaphoreType.DMA,
                pltpu.SemaphoreType.DMA((2,)),
            ],
            alias=alias,
        )

    def pack(name, *parts):
        return kernel(
            pack_body,
            name,
            struct((sum(v.shape[0] for v in parts), parts[0].shape[1]), parts[0].dtype),
            [VMEM] * len(parts),
            VMEM,
            parts,
        )

    def last_rows(i, weight, state, saved, spread, *gradient):
        kinds = [struct((count, width), BF16)]
        scratch = [pltpu.VMEM((count, kept), BF16)]
        if i == 0:
            kinds += [struct((count, columns), F32)]
        else:
            kinds += [struct((count, columns), BF16), struct((ranks, columns), F32)]
            scratch += [pltpu.VMEM((count, columns), BF16), pltpu.VMEM((ranks, columns), F32)]
        operands = [saved[0], cotangent, spread, saved[1], weight, state[1], *gradient, state[0]]
        return kernel(
            functools.partial(last_body, planes - 1, rows, i),
            f"last_rows_{i}",
            kinds,
            [VMEM] * (len(operands) - 1) + [HBM],
            [HBM, VMEM] if i == 0 else [HBM] * 3,
            operands,
            scratch=scratch + [pltpu.SemaphoreType.DMA((1 if i == 0 else 4,))],
            alias={len(operands) - 1: 0},
        )

    def cut(name, v):
        return kernel(
            cut_body, name, struct((kept, columns), BF16), [VMEM], VMEM, (v,)
        )

    core_share = over_core(send)
    z1, spread = hold(z1, spread)
    z2 = over_z(z1)
    y1 = over_y(z1)
    z1, spread = hold(z1, spread)
    cut_z1 = cut("cut_1", z1)
    cut_z1, spread = hold(cut_z1, spread)
    x1a = over_x(cut_z1)
    y0, spread = hold(y0, spread)
    x0 = over_x(y0[:kept])
    core_share, spread = hold(core_share, spread)
    own_y, other_y = kernel(
        core_sum_body,
        "core_sum",
        [struct((planes, each, ranks), F32), struct((planes, each, ranks), BF16)],
        [VMEM] * 2,
        [VMEM] * 2,
        (keep, core_share),
    )
    own_y, spread = hold(own_y, spread)
    side_share = over_y(other_y)
    x1a, spread = hold(x1a, spread)
    y1, spread = hold(y1, spread)
    x1b = over_x(y1[:kept])
    z2, spread = hold(z2, spread)
    z3 = over_z(z2)
    y2 = over_y(z2)
    x2a = over_x(z2[:kept])
    x0, spread = hold(x0, spread)
    side_share, spread = hold(side_share, spread)
    x0, spread = hold(x0, spread)
    pack_0 = pack("pack_0", p0, y0, rest, x0)
    pack_0, spread = hold(pack_0, spread)
    c0 = over_core(pack_0)
    x1b, spread = hold(x1b, spread)
    side_share, spread = hold(side_share, spread)
    line = struct((rows + planes * half, ranks), BF16)
    mine, s1, s2, s3 = kernel(
        functools.partial(side_sum_body, rows),
        "side_sum",
        [struct(line.shape, F32), line, line, line],
        [VMEM] * 2,
        [VMEM] * 4,
        (own_y, side_share),
    )
    mine, spread = hold(mine, spread)
    line_1 = over_z(s1, 1)
    line_2 = over_z(s2, 2)
    line_3 = over_z(s3, 3)
    x1b, spread = hold(x1b, spread)
    pack_1 = pack("pack_1", z1, y1, x1a, x1b)
    pack_1, spread = hold(pack_1, spread)
    c1 = over_core(pack_1)
    z3, spread = hold(z3, spread)
    y3 = over_y(z3)
    x3a = over_x(z3[:kept])
    x2a, spread = hold(x2a, spread)
    c0, spread = hold(c0, spread)
    y2, spread = hold(y2, spread)
    x2b = over_x(y2[:kept])
    line_2, spread = hold(line_2, spread)
    c0, spread = hold(c0, spread)
    act, acc = plane(0, [p0, y0, rest, x0], [c0], None, spread)
    acc, spread = hold(acc, spread)
    c1, spread = hold(c1, spread)
    act, acc = plane(1, [z1, y1, x1a, x1b], [c1], (act, acc), spread)
    acc, spread = hold(acc, spread)
    x3a, spread = hold(x3a, spread)
    y3, spread = hold(y3, spread)
    x3b = over_x(y3[:kept])
    x2b, spread = hold(x2b, spread)
    pack_2 = pack("pack_2", z2, y2, x2a, x2b)
    pack_2, spread = hold(pack_2, spread)
    c2 = over_core(pack_2)
    x3a, spread = hold(x3a, spread)
    pack_3 = pack("pack_3", z3, y3, x3a)
    pack_3, spread = hold(pack_3, spread)
    c3a = over_core(pack_3)
    line_3, spread = hold(line_3, spread)
    line_1, spread = hold(line_1, spread)
    grad_a, quarter = kernel(
        line_sum_body,
        "line_sum",
        [struct((rows, ranks), F32), struct((planes * half, ranks), F32)],
        [VMEM] * 4,
        [VMEM] * 2,
        (mine, line_1, line_2, line_3),
    )
    quarter, spread = hold(quarter, spread)
    side_up = over_y(quarter)
    c2, spread = hold(c2, spread)
    act, acc = plane(2, [z2, y2, x2a, x2b], [c2], (act, acc), spread)
    acc, spread = hold(acc, spread)
    c3a, spread = hold(c3a, spread)
    act, acc, *saved = plane(3, [z3, y3, x3a], [c3a], (act, acc), spread)
    acc, spread = hold(acc, spread)
    side_up, spread = hold(side_up, spread)
    both = pack("pack_up", quarter, side_up)
    both, spread = hold(both, spread)
    core_up = over_core(both)
    x3b, spread = hold(x3b, spread)
    c3b = over_core(x3b)
    act, acc = last_rows(0, x3b, (act, acc), saved, spread)
    acc, spread = hold(acc, spread)
    core_up, spread = hold(core_up, spread)
    c3b, spread = hold(c3b, spread)
    act, values, grad_b = last_rows(1, c3b, (act, acc), saved, spread, both, core_up)
    return values, act, grad_a, grad_b


def solution(mesh):
    sizes = (mesh.shape["groups"], mesh.shape["seq"])

    def on_device(*operands):
        rows, columns = operands[2].shape
        ranks = operands[5].shape[0]
        fits = rows == 5 * STRIP and columns == 8 * ranks
        path = block_path if sizes == (2, 16) and fits and ranks == BLOCK else plain_path
        return path(*operands)

    return jax.shard_map(
        on_device,
        mesh=mesh,
        in_specs=(
            P(("groups", "seq"), None),
            P(("groups", "seq")),
            P("seq", None),
            P(),
            P("groups", None),
            P("groups", None),
            P(("groups", "seq"), None),
        ),
        out_specs=(
            P(("groups", "seq"), None),
            P(("groups", "seq"), None),
            P(("groups", "seq"), None),
            P("groups", None),
        ),
        check_vma=False,
    )
```
